128 devices in a mesh: row: 16 (over z_hi, y, core), col: 8 (over z_lo, x).
Axes of the slice: x: 4, y: 4, z: 4 (z_hi: 2, z_lo: 2; z = z_hi * 2 + z_lo), core: 2. Of those that a mesh axis runs over, the one named last changes fastest.
Arguments:
- node_features: bfloat16 [32768, 128], P(('row', 'col')), may hold values from -6 to 6
- tile_values: bfloat16 [16, 8, 384, 128, 128], P('row', 'col'), may hold values from -0.109375 to 0.109375
- tile_rows: int32 [16, 8, 384], P('row', 'col'), may hold values from 0 to 15
- tile_cols: int32 [16, 8, 384], P('row', 'col'), may hold values from 0 to 31
- tile_count: int32 [16, 8], P('row', 'col'), may hold values from 48 to 384, as said below
- labels: int32 [32768], P(('row', 'col')), may hold values from 0 to 46
- train_mask: int32 [32768], P(('row', 'col')), may hold values from 0 to 1, as said below
- hidden_weight: bfloat16 [128, 256], replicated, may hold values from -0.5 to 0.5
- hidden_bias: float32 [256], replicated, may hold values from -3 to 3
- class_weight: bfloat16 [256, 47], replicated, may hold values from -3.59375 to 3.59375
- class_bias: float32 [47], replicated, may hold values from -4 to 4
Outputs:
- hidden: bfloat16 [32768, 256], P(('row', 'col'))
- logits: float32 [47, 32768], P(None, ('row', 'col'))
- mean_loss: float32 [], replicated
- hidden_weight_grad: float32 [128, 256], replicated
- hidden_bias_grad: float32 [256], replicated
- class_weight_grad: float32 [256, 47], replicated
- class_bias_grad: float32 [47], replicated
The draws below stay inside these ranges and needn't reach their ends.
Inputs may be any that keep to these rules, and one draw needn't show every extreme that they name: Slots s >= tile_count of a block are not part of it; some block has all 384 slots live. `train_mask`: at least one node is a training node.
All inputs are finite; a program needn't handle non-finite values.
Results may differ from the reference program's by a relative error of at most 0.025.
Values may be sent and summed in bfloat16 or wider, within the bound.
A program may use at most 128 MiB of HBM per device.

```python
import jax
import jax.numpy as jnp
from jax import lax

F_IN = 128
HIDDEN_SIZE = 256
CLASSES = 47
TILE = 128
NODES_DEV = 256
TILES_DEV = 384
NODES = 32768
N_ROW = 16
N_COL = 8


def draw_tile_count(key, part):
    lowest = max(1, TILES_DEV // 8)
    highest = max(TILES_DEV // 2 + 1, lowest + 1)
    positions = N_ROW * N_COL
    counts = jax.random.randint(key, (positions,), lowest, highest)
    chosen = jax.random.randint(jax.random.fold_in(key, 7), (), 0, positions)
    counts = jnp.where(jnp.arange(positions) == chosen, TILES_DEV, counts)
    return counts.reshape(N_ROW, N_COL).astype(jnp.int32)


def draw_train_mask(key, part):
    slices = jnp.arange(NODES) // NODES_DEV
    positions = N_ROW * N_COL
    chance = 150 + 300 * slices // max(positions - 1, 1)
    rolled = jax.random.randint(key, (NODES,), 0, 1000)
    marked = (rolled < chance).astype(jnp.int32)
    return marked.at[0].set(1).astype(jnp.int32)


def place_ends(result, stream_key, least, high):
    place = [jax.random.randint(jax.random.fold_in(stream_key, axis), (), 0, length) for axis, length in enumerate(result.shape)]
    longest = result.shape.index(max(result.shape))
    neighbour = place[:longest] + [(place[longest] + 1) % result.shape[longest]] + place[longest + 1:]
    return result.at[tuple(place)].set(least).at[tuple(neighbour)].set(high)


def steps_of(own_key, extent, cuts, low, largest):
    level = 1.0
    for dim, shards_of in cuts:
        draws = jax.random.uniform(jax.random.fold_in(jax.random.fold_in(own_key, 6), dim), (shards_of,), jnp.float32, low / len(cuts), largest / len(cuts))
        level = level * jnp.repeat(jnp.exp(draws), extent[dim] // shards_of).reshape((-1,) + (1,) * (len(extent) - 1 - dim))
    return level


def normal_values(key, extent, spread, bound, split=(), kind=jnp.bfloat16):
    array = spread * jax.random.normal(key, extent, jnp.float32)
    if split:
        array = array * steps_of(key, extent, split, -0.22, 0.18)
    return jnp.clip(array, -bound, bound).astype(kind)


def setup_inputs(seed: int = 0) -> dict:
    key_list = jax.random.split(jax.random.key(seed), 12)
    return {
        "node_features": normal_values(key_list[0], (NODES, F_IN), 1.0, 6.0, ((0, 128),)),
        "tile_values": normal_values(key_list[1], (N_ROW, N_COL, TILES_DEV, TILE, TILE), (TILE * TILE * TILES_DEV // (N_COL * NODES_DEV)) ** -0.5, 0.109375, ((0, 16), (1, 8))),
        "tile_rows": place_ends(jax.random.randint(key_list[2], (N_ROW, N_COL, TILES_DEV), 0, N_COL * NODES_DEV // TILE), jax.random.fold_in(key_list[2], 1), 0, (N_COL * NODES_DEV // TILE) - 1).astype(jnp.int32),
        "tile_cols": place_ends(jax.random.randint(key_list[3], (N_ROW, N_COL, TILES_DEV), 0, N_ROW * NODES_DEV // TILE), jax.random.fold_in(key_list[3], 1), 0, (N_ROW * NODES_DEV // TILE) - 1).astype(jnp.int32),
        "tile_count": draw_tile_count(jax.random.fold_in(key_list[11], 71), 0),
        "labels": place_ends(jax.random.randint(key_list[5], (NODES,), 0, CLASSES), jax.random.fold_in(key_list[5], 1), 0, CLASSES - 1).astype(jnp.int32),
        "train_mask": draw_train_mask(jax.random.fold_in(key_list[11], 71), 0),
        "hidden_weight": normal_values(key_list[7], (F_IN, HIDDEN_SIZE), F_IN ** -0.5, 0.5),
        "hidden_bias": normal_values(key_list[8], (HIDDEN_SIZE,), 0.5, 3.0, (), jnp.float32),
        "class_weight": normal_values(key_list[9], (HIDDEN_SIZE, CLASSES), 0.6, 3.59375),
        "class_bias": normal_values(key_list[10], (CLASSES,), 1.0, 4.0, (), jnp.float32),
    }


def block_product(values, tile_rows, tile_cols, tile_total, source, out_tiles, transpose):
    feature_width = source.shape[1]
    tiled = source.reshape(-1, TILE, feature_width).astype(jnp.float32)
    if transpose:
        pieces = tiled[tile_rows]
        product = jnp.einsum("gji,gjf->gif", values.astype(jnp.float32), pieces, precision=lax.Precision.HIGHEST)
        target = tile_cols
    else:
        pieces = tiled[tile_cols]
        product = jnp.einsum("gij,gjf->gif", values.astype(jnp.float32), pieces, precision=lax.Precision.HIGHEST)
        target = tile_rows
    live_slots = (jnp.arange(TILES_DEV) < tile_total).astype(jnp.float32)
    product = product * live_slots[:, None, None]
    summed = jax.ops.segment_sum(product, target, num_segments=out_tiles)
    return summed.reshape(out_tiles * TILE, feature_width)


def rounded(term):
    return lax.optimization_barrier(term.astype(jnp.bfloat16)).astype(jnp.float32)


def aggregate(source, tile_values, tile_rows, tile_cols, tile_count, round_terms):
    feature_width = source.shape[1]
    grid = source.reshape(N_ROW, N_COL, NODES_DEV, feature_width)

    def one_row(row_index):
        def add_col(total, col_index):
            column_block = grid[:, col_index].reshape(N_ROW * NODES_DEV, feature_width)
            term = block_product(tile_values[row_index, col_index], tile_rows[row_index, col_index], tile_cols[row_index, col_index], tile_count[row_index, col_index], column_block, N_COL * NODES_DEV // TILE, False)
            if round_terms:
                term = rounded(term)
            return total + term, None

        start = jnp.zeros((N_COL * NODES_DEV, feature_width), jnp.float32)
        total, _ = lax.scan(add_col, start, jnp.arange(N_COL))
        return total

    return lax.map(one_row, jnp.arange(N_ROW)).reshape(NODES, feature_width)


def aggregate_back(source, tile_values, tile_rows, tile_cols, tile_count):
    feature_width = source.shape[1]
    grid = source.reshape(N_ROW, N_COL * NODES_DEV, feature_width)

    def one_col(col_index):
        def add_row(total, row_index):
            term = block_product(tile_values[row_index, col_index], tile_rows[row_index, col_index], tile_cols[row_index, col_index], tile_count[row_index, col_index], grid[row_index], N_ROW * NODES_DEV // TILE, True)
            return total + term, None

        start = jnp.zeros((N_ROW * NODES_DEV, feature_width), jnp.float32)
        total, _ = lax.scan(add_row, start, jnp.arange(N_ROW))
        return total

    columns = lax.map(one_col, jnp.arange(N_COL))
    return columns.reshape(N_COL, N_ROW, NODES_DEV, feature_width).transpose(1, 0, 2, 3).reshape(NODES, feature_width)


def reference(node_features, tile_values, tile_rows, tile_cols, tile_count, labels, train_mask, hidden_weight, hidden_bias, class_weight, class_bias):
    first_agg = aggregate(node_features, tile_values, tile_rows, tile_cols, tile_count, True).astype(jnp.bfloat16)
    hidden_pre = jnp.dot(first_agg, hidden_weight, preferred_element_type=jnp.float32) + hidden_bias
    hidden = jax.nn.silu(hidden_pre).astype(jnp.bfloat16)
    second_agg = aggregate(hidden, tile_values, tile_rows, tile_cols, tile_count, False)
    class_weight_wide = class_weight.astype(jnp.float32)
    logits = jnp.einsum("hk,nh->kn", class_weight_wide, second_agg, precision=lax.Precision.HIGHEST) + class_bias[:, None]
    top = jnp.max(logits, axis=0)
    log_total = top + jnp.log(jnp.sum(jnp.exp(logits - top[None, :]), axis=0))
    onehot = (jnp.arange(CLASSES)[:, None] == labels[None, :]).astype(jnp.float32)
    cross_entropy = log_total - jnp.sum(onehot * logits, axis=0)
    weights = train_mask.astype(jnp.float32)
    count = jnp.sum(weights)
    mean_loss = jnp.sum(weights * cross_entropy) / count
    class_grad = (jnp.exp(logits - log_total[None, :]) - onehot) * (weights / count)[None, :]
    class_weight_grad = jnp.einsum("nh,kn->hk", second_agg, class_grad, precision=lax.Precision.HIGHEST)
    class_bias_grad = jnp.sum(class_grad, axis=1)
    agg_grad = jnp.einsum("kn,hk->nh", class_grad, class_weight_wide, precision=lax.Precision.HIGHEST)
    hidden_grad = aggregate_back(agg_grad, tile_values, tile_rows, tile_cols, tile_count)
    sigma = jax.nn.sigmoid(hidden_pre)
    pre_grad = hidden_grad * sigma * (1.0 + hidden_pre * (1.0 - sigma))
    hidden_weight_grad = jnp.einsum("nf,nh->fh", first_agg.astype(jnp.float32), pre_grad, precision=lax.Precision.HIGHEST)
    hidden_bias_grad = jnp.sum(pre_grad, axis=0)
    return (hidden, logits, mean_loss, hidden_weight_grad, hidden_bias_grad, class_weight_grad, class_bias_grad)
```

```python
import jax
import jax.numpy as jnp
from jax import lax
from jax.experimental import pallas as pl
from jax.experimental.pallas import tpu as pltpu
from jax.sharding import PartitionSpec as P

TILE = 128
PADDED = 48
NT = (((1,), (1,)), ((), ()))
TN = (((0,), (0,)), ((), ()))


def densify_kernel(n_rows, rows, cols, count, values, out, head, nxt, dups, sem):
    slots = values.shape[0]
    places = out.shape[0] - slots
    live = count[0, 0]
    zero = jnp.zeros((TILE, TILE), jnp.bfloat16)

    def clear(p, _):
        head[p] = -1
        out[p] = zero
        return 0

    lax.fori_loop(0, places, clear, 0, unroll=8)

    def place(s, found):
        p = cols[s] * n_rows + rows[s]
        alive = s < live
        before = head[p]
        first = jnp.logical_and(alive, before < 0)
        again = jnp.logical_and(alive, before >= 0)
        head[p] = jnp.where(alive, s, before)
        nxt[s] = before
        dups[found] = p
        pltpu.make_async_copy(
            values.at[s], out.at[jnp.where(first, p, places + s)], sem
        ).start()
        return found + again.astype(jnp.int32)

    found = lax.fori_loop(0, slots, place, 0, unroll=8)
    pltpu.make_async_copy(values, out.at[pl.ds(places, slots)], sem).wait()

    def merge(i, _):
        p = dups[i]
        top = head[p]

        @pl.when(top >= 0)
        def _():
            head[p] = -1

            def more(state):
                return nxt[state[0]] >= 0

            def add(state):
                s, total = state
                return nxt[s], total + out[places + s].astype(jnp.float32)

            _, total = lax.while_loop(more, add, (top, out[p].astype(jnp.float32)))
            out[p] = total.astype(jnp.bfloat16)

        return 0

    lax.fori_loop(0, found, merge, 0)


def densify(rows, cols, count, values, n_rows, n_cols):
    slots = values.shape[0]
    places = n_rows * n_cols
    smem = pl.BlockSpec(memory_space=pltpu.SMEM)
    return pl.pallas_call(
        lambda *refs: densify_kernel(n_rows, *refs),
        out_shape=pltpu.VMEM((places + slots, TILE, TILE), jnp.bfloat16),
        in_specs=[smem, smem, smem, pl.BlockSpec(memory_space=pltpu.HBM)],
        out_specs=pl.BlockSpec(memory_space=pltpu.VMEM),
        scratch_shapes=[
            pltpu.SMEM((places,), jnp.int32),
            pltpu.SMEM((slots,), jnp.int32),
            pltpu.SMEM((slots + 1,), jnp.int32),
            pltpu.SemaphoreType.DMA,
        ],
        compiler_params=pltpu.CompilerParams(vmem_limit_bytes=4 * 2**20),
        name="densify",
    )(rows, cols, count, values)


def square(dense, row_chunk, col_chunk, n_rows):
    halves = [
        dense[pl.ds((2 * col_chunk + h) * n_rows + 2 * row_chunk, 2)].reshape(2 * TILE, TILE)
        for h in range(2)
    ]
    return jnp.concatenate(halves, axis=1)


def first_kernel(n_rows, dense, source, out):
    def one_chunk(i, _):
        total = jnp.zeros((2 * TILE, source.shape[1]), jnp.float32)
        for k in range(source.shape[0] // (2 * TILE)):
            piece = source[k * 2 * TILE : (k + 1) * 2 * TILE, :]
            total += jnp.dot(
                square(dense, i, k, n_rows), piece, preferred_element_type=jnp.float32
            )
        out[pl.ds(i * 2 * TILE, 2 * TILE), :] = total.astype(out.dtype)
        return 0

    lax.fori_loop(0, n_rows // 2, one_chunk, 0)


def second_kernel(n_rows, dense, source, out):
    def one_chunk(i, _):
        total = jnp.zeros(out.shape[1:], jnp.float32)
        for k in range(source.shape[0]):
            total += lax.dot_general(
                source[k], square(dense, i, k, n_rows), NT, preferred_element_type=jnp.float32
            )
        out[i] = total.astype(out.dtype)
        return 0

    lax.fori_loop(0, n_rows // 2, one_chunk, 0)


def back_kernel(n_rows, dense, source, out):
    def one_chunk(k, _):
        total = jnp.zeros(out.shape[1:], jnp.float32)
        for i in range(source.shape[0]):
            total += jnp.dot(
                source[i], square(dense, i, k, n_rows), preferred_element_type=jnp.float32
            )
        out[k] = total.astype(out.dtype)
        return 0

    lax.fori_loop(0, out.shape[0], one_chunk, 0)


def on_dense(kernel, n_rows, dense, source, shape, name):
    vmem = pl.BlockSpec(memory_space=pltpu.VMEM)
    return pl.pallas_call(
        lambda *refs: kernel(n_rows, *refs),
        out_shape=jax.ShapeDtypeStruct(shape, jnp.bfloat16),
        in_specs=[vmem, vmem],
        out_specs=vmem,
        compiler_params=pltpu.CompilerParams(vmem_limit_bytes=12 * 2**20),
        name=name,
    )(pltpu.with_memory_space_constraint(dense, pltpu.VMEM), source)


def on_device(
    node_features,
    tile_values,
    tile_rows,
    tile_cols,
    tile_count,
    labels,
    train_mask,
    hidden_weight,
    hidden_bias,
    class_weight,
    class_bias,
):
    nodes = node_features.shape[0]
    classes = class_bias.shape[0]
    row_size, col_size = lax.axis_size("row"), lax.axis_size("col")
    n_rows, n_cols = col_size * nodes // TILE, row_size * nodes // TILE
    dense = densify(tile_rows[0, 0], tile_cols[0, 0], tile_count, tile_values[0, 0], n_rows, n_cols)
    gathered = lax.all_gather(node_features, "row", axis=0, tiled=True)
    first_term = on_dense(
        first_kernel, n_rows, dense, gathered, (n_rows * TILE, gathered.shape[1]), "first"
    )
    first_agg = lax.psum_scatter(first_term, "col", scatter_dimension=0, tiled=True)
    hidden_pre = (
        jnp.dot(first_agg, hidden_weight, preferred_element_type=jnp.float32) + hidden_bias
    )
    hidden = jax.nn.silu(hidden_pre).astype(jnp.bfloat16)
    weight = jnp.pad(class_weight, ((0, 0), (0, PADDED - classes)))
    score_part = lax.dot_general(
        weight, hidden, (((0,), (1,)), ((), ())), preferred_element_type=jnp.float32
    ).astype(jnp.bfloat16)
    parts = lax.all_gather(score_part, "row", axis=0)
    second_term = on_dense(second_kernel, n_rows, dense, parts, (col_size, PADDED, nodes), "second")
    scores = lax.psum_scatter(second_term, "col", scatter_dimension=0)
    logits = scores[:classes].astype(jnp.float32) + class_bias[:, None]
    top = jnp.max(logits, axis=0)
    log_total = top + jnp.log(jnp.sum(jnp.exp(logits - top[None, :]), axis=0))
    onehot = (jnp.arange(classes)[:, None] == labels[None, :]).astype(jnp.float32)
    cross_entropy = log_total - jnp.sum(onehot * logits, axis=0)
    weights = train_mask.astype(jnp.float32)
    class_grad = (jnp.exp(logits - log_total[None, :]) - onehot) * weights[None, :]
    grad = jnp.pad(class_grad, ((0, PADDED - classes), (0, 0))).astype(jnp.bfloat16)
    grads = lax.all_gather(grad, "col", axis=0)
    back_term = on_dense(back_kernel, n_rows, dense, grads, (row_size, PADDED, nodes), "back")
    back = lax.psum_scatter(back_term, "row", scatter_dimension=0)
    hidden_grad = lax.dot_general(
        back, weight, (((0,), (1,)), ((), ())), preferred_element_type=jnp.float32
    )
    sigma = jax.nn.sigmoid(hidden_pre)
    pre_grad = hidden_grad * sigma * (1.0 + hidden_pre * (1.0 - sigma))
    hidden_weight_part = lax.dot_general(
        first_agg, pre_grad.astype(jnp.bfloat16), TN, preferred_element_type=jnp.float32
    )
    class_weight_part = lax.dot_general(
        hidden, back[:classes], TN_CLASS, preferred_element_type=jnp.float32
    )
    sums = lax.psum(
        (
            hidden_weight_part,
            jnp.sum(pre_grad, axis=0),
            class_weight_part,
            jnp.sum(class_grad, axis=1),
            jnp.sum(weights * cross_entropy),
            jnp.sum(weights),
        ),
        ("row", "col"),
    )
    count = sums[5]
    return (
        hidden,
        logits,
        sums[4] / count,
        sums[0] / count,
        sums[1] / count,
        sums[2] / count,
        sums[3] / count,
    )


TN_CLASS = (((0,), (1,)), ((), ()))


def solution(mesh):
    in_specs = (
        P(("row", "col"), None),
        P("row", "col", None, None, None),
        P("row", "col", None),
        P("row", "col", None),
        P("row", "col"),
        P(("row", "col")),
        P(("row", "col")),
        P(),
        P(),
        P(),
        P(),
    )
    out_specs = (P(("row", "col"), None), P(None, ("row", "col")), P(), P(), P(), P(), P())
    return jax.shard_map(
        on_device, mesh=mesh, in_specs=in_specs, out_specs=out_specs, check_vma=False
    )
```

```python
import jax
import jax.numpy as jnp
from jax import lax
from jax.experimental import pallas as pl
from jax.experimental.pallas import tpu as pltpu
from jax.sharding import PartitionSpec as P

TILE = 128
PADDED = 48
MESH = pl.DeviceIdType.MESH
NT = (((1,), (1,)), ((), ()))
TN = (((0,), (0,)), ((), ()))


def densify_kernel(n_rows, rows, cols, count, values, out, head, nxt, dups, sem):
    slots = values.shape[0]
    places = out.shape[0] - slots
    live = count[0, 0]
    zero = jnp.zeros((TILE, TILE), jnp.bfloat16)

    def clear(p, _):
        head[p] = -1
        out[p] = zero
        return 0

    lax.fori_loop(0, places, clear, 0, unroll=8)

    def place(s, found):
        p = cols[0, 0, s] * n_rows + rows[0, 0, s]
        alive = s < live
        before = head[p]
        first = jnp.logical_and(alive, before < 0)
        again = jnp.logical_and(alive, before >= 0)
        head[p] = jnp.where(alive, s, before)
        nxt[s] = before
        dups[found] = p
        pltpu.make_async_copy(
            values.at[s], out.at[jnp.where(first, p, places + s)], sem
        ).start()
        return found + again.astype(jnp.int32)

    found = lax.fori_loop(0, slots, place, 0, unroll=8)
    pltpu.make_async_copy(values, out.at[pl.ds(places, slots)], sem).wait()

    def merge(i, _):
        p = dups[i]
        top = head[p]

        @pl.when(top >= 0)
        def _():
            head[p] = -1

            def more(state):
                return nxt[state[0]] >= 0

            def add(state):
                s, total = state
                return nxt[s], total + out[places + s].astype(jnp.float32)

            _, total = lax.while_loop(more, add, (top, out[p].astype(jnp.float32)))
            out[p] = total.astype(jnp.bfloat16)

        return 0

    lax.fori_loop(0, found, merge, 0)


def densify(rows, cols, count, values, n_rows, n_cols):
    slots = values.shape[0]
    places = n_rows * n_cols
    smem = pl.BlockSpec(memory_space=pltpu.SMEM)
    return pl.pallas_call(
        lambda *refs: densify_kernel(n_rows, *refs),
        out_shape=pltpu.VMEM((places + slots, TILE, TILE), jnp.bfloat16),
        in_specs=[smem, smem, smem, pl.BlockSpec(memory_space=pltpu.HBM)],
        out_specs=pl.BlockSpec(memory_space=pltpu.VMEM),
        scratch_shapes=[
            pltpu.SMEM((places,), jnp.int32),
            pltpu.SMEM((slots,), jnp.int32),
            pltpu.SMEM((slots + 1,), jnp.int32),
            pltpu.SemaphoreType.DMA,
        ],
        compiler_params=pltpu.CompilerParams(vmem_limit_bytes=4 * 2**20),
        name="densify",
    )(rows, cols, count, pltpu.with_memory_space_constraint(values, pltpu.HBM))


class Exchange:
    def __init__(self, axis, size, dst, send_sem, recv_sem):
        self.axis, self.size, self.dst = axis, size, dst
        self.send_sem, self.recv_sem = send_sem, recv_sem
        self.me = lax.axis_index(axis)

    def copy(self, source, slot, peer):
        return pltpu.make_async_remote_copy(
            src_ref=source,
            dst_ref=self.dst.at[slot],
            send_sem=self.send_sem.at[peer],
            recv_sem=self.recv_sem.at[slot],
            device_id={self.axis: peer},
            device_id_type=MESH,
        )

    def peers(self, body):
        def step(d, _):
            body(lax.rem(self.me + d, self.size))
            return 0

        lax.fori_loop(1, self.size, step, 0)

    def send(self, source, peer):
        self.copy(source, self.me, peer).start()

    def send_all(self, source_of):
        self.peers(lambda peer: self.send(source_of(peer), peer))

    def receive_all(self):
        self.peers(lambda peer: self.copy(self.dst.at[peer], peer, peer).wait_recv())

    def sent_all(self):
        self.peers(lambda peer: self.copy(self.dst.at[peer], self.me, peer).wait_send())


def rows_of(dense, i, n_rows, n_cols):
    return jnp.concatenate(
        [dense[pl.ds(k * n_rows + 2 * i, 2)].reshape(2 * TILE, TILE) for k in range(n_cols)],
        axis=1,
    )


def cols_of(dense, k, n_rows):
    return jnp.concatenate(
        [
            dense[pl.ds((2 * k + h) * n_rows, n_rows)].reshape(n_rows * TILE, TILE)
            for h in range(2)
        ],
        axis=1,
    )


def step_kernel(
    R,
    C,
    x,
    dense,
    labels,
    mask,
    w1,
    b1,
    w2,
    b2,
    hidden_out,
    logits_out,
    loss_out,
    w1_grad_out,
    b1_grad_out,
    w2_grad_out,
    b2_grad_out,
    xg,
    t1,
    r1,
    s2,
    hw,
    t2,
    r2,
    s3,
    gg,
    t3,
    r3,
    part,
    r4,
    s5,
    r5,
    fin,
    pre,
    agg,
    w2s,
    b2s,
    send_sems,
    recv_sems,
):
    n_rows, n_cols = 2 * C, 2 * R
    nodes = x.shape[0]
    classes = w2.shape[0]
    piece = fin.shape[1]
    row, col = lax.axis_index("row"), lax.axis_index("col")

    barrier = pltpu.get_barrier_semaphore()

    def greet(axis, me, size):
        def one(d, _):
            pl.semaphore_signal(
                barrier,
                inc=1,
                device_id={axis: lax.rem(me + d, size)},
                device_id_type=MESH,
            )
            return 0

        lax.fori_loop(1, size, one, 0)

    greet("row", row, R)
    greet("col", col, C)

    def exchange(number, axis, size, dst):
        return Exchange(axis, size, dst, send_sems.at[number], recv_sems.at[number])

    ex_x = exchange(0, "row", R, xg)
    ex_first = exchange(1, "col", C, r1)
    ex_hw = exchange(2, "row", R, hw)
    ex_second = exchange(3, "col", C, r2)
    ex_grad = exchange(4, "col", C, gg)
    ex_back = exchange(5, "row", R, r3)
    ex_part = exchange(6, "row", R, r4)
    ex_sum = exchange(7, "col", C, r5)
    ex_fin = exchange(8, "row", R, fin)

    xg[row] = x[...]
    w2s[...] = jnp.zeros_like(w2s)
    w2s[0:classes, :] = w2[...].astype(jnp.float32)
    b2s[...] = jnp.zeros_like(b2s)
    b2s[0:1, 0:classes] = b2[...]
    pl.semaphore_wait(barrier, R + C - 2)

    ex_x.send_all(lambda peer: x)
    ex_x.receive_all()

    source = xg.reshape(R * nodes, x.shape[1])

    def first(d, _):
        peer = lax.rem(col + d, C)
        t1[peer] = jnp.dot(
            rows_of(dense, peer, n_rows, n_cols), source[...], preferred_element_type=jnp.float32
        ).astype(t1.dtype)

        @pl.when(d < C)
        def _():
            ex_first.send(t1.at[peer], peer)

        return 0

    lax.fori_loop(1, C + 1, first, 0)
    r1[col] = t1[col]
    ex_first.receive_all()

    def add_up(ref, size):
        return lax.fori_loop(
            1,
            size,
            lambda j, total: total + ref[j].astype(jnp.float32),
            ref[0].astype(jnp.float32),
        )

    agg[...] = add_up(r1, C).astype(jnp.bfloat16)
    v = jnp.dot(agg[...], w1[...], preferred_element_type=jnp.float32) + b1[...]
    pre[...] = v
    hidden_out[...] = (v / (1.0 + jnp.exp(-v))).astype(jnp.bfloat16)
    s2[...] = lax.dot_general(
        w2s[...].astype(jnp.bfloat16), hidden_out[...], NT, preferred_element_type=jnp.float32
    ).astype(jnp.bfloat16)

    hw[row] = s2[...]
    ex_hw.send_all(lambda peer: s2)
    ex_hw.receive_all()

    def second(d, _):
        peer = lax.rem(col + d, C)
        left = jnp.concatenate([hw[k] for k in range(R)], axis=1)
        t2[peer] = lax.dot_general(
            left, rows_of(dense, peer, n_rows, n_cols), NT, preferred_element_type=jnp.float32
        ).astype(t2.dtype)

        @pl.when(d < C)
        def _():
            ex_second.send(t2.at[peer], peer)

        return 0

    lax.fori_loop(1, C + 1, second, 0)
    r2[col] = t2[col]
    ex_second.receive_all()

    turned = jnp.transpose(jnp.broadcast_to(b2s[0:1, :], (TILE, TILE)))[0:PADDED, :]
    logits = add_up(r2, C) + jnp.concatenate([turned] * (nodes // TILE), axis=1)
    logits_out[...] = logits[0:classes, :]
    index = lax.broadcasted_iota(jnp.int32, (PADDED, nodes), 0)
    real = index < classes
    top = jnp.max(jnp.where(real, logits, -jnp.inf), axis=0, keepdims=True)
    terms = jnp.where(real, jnp.exp(logits - top), 0.0)
    log_total = top + jnp.log(jnp.sum(terms, axis=0, keepdims=True))
    onehot = (index == labels[...]).astype(jnp.float32)
    weights = mask[...].astype(jnp.float32)
    cross = weights * (log_total - jnp.sum(onehot * logits, axis=0, keepdims=True))
    grad = jnp.where(real, jnp.exp(logits - log_total) - onehot, 0.0) * weights
    s3[...] = grad.astype(jnp.bfloat16)

    gg[col] = s3[...]
    ex_grad.send_all(lambda peer: s3)

    def halves(base, value):
        height = value.shape[0]
        for h in range(2):
            part[pl.ds(base + h * height, height), :] = value[:, h * TILE : (h + 1) * TILE]

    base2, base3 = 2 * w1.shape[0], 2 * w1.shape[0] + 2 * PADDED
    ones = jnp.ones((8, nodes), jnp.float32)
    b2_part = lax.dot_general(
        ones, grad, NT, precision=lax.Precision.HIGHEST, preferred_element_type=jnp.float32
    )
    part[pl.ds(base3, 32), :] = jnp.zeros((32, TILE), jnp.float32)
    part[pl.ds(base3 + 8, 1), 0:PADDED] = b2_part[0:1, :]
    part[pl.ds(base3 + 16, 1), :] = jnp.broadcast_to(
        jnp.sum(cross, axis=1, keepdims=True), (1, TILE)
    )
    part[pl.ds(base3 + 24, 1), :] = jnp.broadcast_to(
        jnp.sum(weights, axis=1, keepdims=True), (1, TILE)
    )
    ex_grad.receive_all()

    def back(d, _):
        peer = lax.rem(row + d, R)
        left = jnp.concatenate([gg[k] for k in range(C)], axis=1)
        t3[peer] = jnp.dot(
            left, cols_of(dense, peer, n_rows), preferred_element_type=jnp.float32
        ).astype(t3.dtype)

        @pl.when(d < R)
        def _():
            ex_back.send(t3.at[peer], peer)

        return 0

    lax.fori_loop(1, R + 1, back, 0)
    r3[row] = t3[row]
    ex_back.receive_all()

    turned_grad = add_up(r3, R).astype(jnp.bfloat16)
    hidden_grad = lax.dot_general(
        turned_grad, w2s[...].astype(jnp.bfloat16), TN, preferred_element_type=jnp.float32
    )
    v = pre[...]
    s = 1.0 / (1.0 + jnp.exp(-v))
    pre_grad = hidden_grad * s * (1.0 + v * (1.0 - s))
    b1_part = jnp.sum(pre_grad, axis=0, keepdims=True)
    for h in range(2):
        part[pl.ds(base3 + h, 1), :] = b1_part[:, h * TILE : (h + 1) * TILE]
    halves(
        0,
        lax.dot_general(
            agg[...], pre_grad.astype(jnp.bfloat16), TN, preferred_element_type=jnp.float32
        ),
    )
    halves(
        base2,
        jnp.dot(turned_grad, hidden_out[...], preferred_element_type=jnp.float32),
    )

    ex_part.send_all(lambda peer: part.at[pl.ds(peer * piece, piece)])
    r4[row] = part[pl.ds(row * piece, piece), :]
    ex_part.receive_all()
    s5[...] = add_up(r4, R)
    r5[col] = s5[...]
    ex_sum.send_all(lambda peer: s5)
    ex_sum.receive_all()
    s5_total = add_up(r5, C)
    fin[row] = s5_total
    ex_fin.send_all(lambda peer: fin.at[row])
    ex_fin.receive_all()

    whole = fin.reshape(R * piece, TILE)
    count = whole[base3 + 24 : base3 + 25, 0:1]
    for h in range(2):
        lanes = slice(h * TILE, (h + 1) * TILE)
        height = w1.shape[0]
        w1_grad_out[:, lanes] = whole[h * height : (h + 1) * height, :] / count
        low = base2 + h * PADDED
        w2_grad_out[:, lanes] = whole[low : low + classes, :] / count
        b1_grad_out[:, lanes] = whole[base3 + h : base3 + h + 1, :] / count
    b2_grad_out[...] = whole[base3 + 8 : base3 + 9, 0:classes] / count
    loss_out[...] = whole[base3 + 16 : base3 + 17, 0:1] / count

    for ex in (ex_x, ex_first, ex_hw, ex_second, ex_grad, ex_back, ex_part, ex_sum, ex_fin):
        ex.sent_all()


def on_device(
    node_features,
    tile_values,
    tile_rows,
    tile_cols,
    tile_count,
    labels,
    train_mask,
    hidden_weight,
    hidden_bias,
    class_weight,
    class_bias,
):
    nodes, features = node_features.shape
    hidden, classes = class_weight.shape
    R, C = lax.axis_size("row"), lax.axis_size("col")
    n_rows, n_cols = C * nodes // TILE, R * nodes // TILE
    dense = densify(tile_rows, tile_cols, tile_count, tile_values[0, 0], n_rows, n_cols)
    used = 2 * features + 2 * PADDED + 32
    piece = -(-used // (8 * R)) * 8
    vmem = pl.BlockSpec(memory_space=pltpu.VMEM)
    bf16, f32 = jnp.bfloat16, jnp.float32
    out = lambda shape, kind: jax.ShapeDtypeStruct(shape, kind)
    scratch = [
        pltpu.VMEM((R, nodes, features), bf16),
        pltpu.VMEM((C, nodes, features), bf16),
        pltpu.VMEM((C, nodes, features), bf16),
        pltpu.VMEM((PADDED, nodes), bf16),
        pltpu.VMEM((R, PADDED, nodes), bf16),
        pltpu.VMEM((C, PADDED, nodes), bf16),
        pltpu.VMEM((C, PADDED, nodes), bf16),
        pltpu.VMEM((PADDED, nodes), bf16),
        pltpu.VMEM((C, PADDED, nodes), bf16),
        pltpu.VMEM((R, PADDED, nodes), bf16),
        pltpu.VMEM((R, PADDED, nodes), bf16),
        pltpu.VMEM((R * piece, TILE), f32),
        pltpu.VMEM((R, piece, TILE), f32),
        pltpu.VMEM((piece, TILE), f32),
        pltpu.VMEM((C, piece, TILE), f32),
        pltpu.VMEM((R, piece, TILE), f32),
        pltpu.VMEM((nodes, hidden), f32),
        pltpu.VMEM((nodes, features), bf16),
        pltpu.VMEM((PADDED, hidden), f32),
        pltpu.VMEM((8, TILE), f32),
        pltpu.SemaphoreType.DMA((9, R)),
        pltpu.SemaphoreType.DMA((9, R)),
    ]
    hidden_out, logits, loss, w1_grad, b1_grad, w2_grad, b2_grad = pl.pallas_call(
        lambda *refs: step_kernel(R, C, *refs),
        out_shape=(
            out((nodes, hidden), bf16),
            out((classes, nodes), f32),
            out((1, 1), f32),
            out((features, hidden), f32),
            out((1, hidden), f32),
            out((classes, hidden), f32),
            out((1, classes), f32),
        ),
        in_specs=[vmem] * 8,
        out_specs=(vmem,) * 7,
        scratch_shapes=scratch,
        compiler_params=pltpu.CompilerParams(
            collective_id=0, has_side_effects=True, vmem_limit_bytes=24 * 2**20
        ),
        name="step",
    )(
        node_features,
        pltpu.with_memory_space_constraint(dense, pltpu.VMEM),
        labels.reshape(1, nodes),
        train_mask.reshape(1, nodes),
        hidden_weight,
        hidden_bias.reshape(1, hidden),
        class_weight.T,
        class_bias.reshape(1, classes),
    )
    return (
        hidden_out,
        logits,
        loss[0, 0],
        w1_grad,
        b1_grad[0],
        w2_grad.T,
        b2_grad[0],
    )


def solution(mesh):
    in_specs = (
        P(("row", "col"), None),
        P("row", "col", None, None, None),
        P("row", "col", None),
        P("row", "col", None),
        P("row", "col"),
        P(("row", "col")),
        P(("row", "col")),
        P(),
        P(),
        P(),
        P(),
    )
    out_specs = (P(("row", "col"), None), P(None, ("row", "col")), P(), P(), P(), P(), P())
    return jax.shard_map(
        on_device, mesh=mesh, in_specs=in_specs, out_specs=out_specs, check_vma=False
    )
```

```python
import jax
import jax.numpy as jnp
from jax import lax
from jax.experimental import pallas as pl
from jax.experimental.pallas import tpu as pltpu
from jax.sharding import PartitionSpec as P

TILE = 128
PADDED = 48
MESH = pl.DeviceIdType.MESH
NT = (((1,), (1,)), ((), ()))
TN = (((0,), (0,)), ((), ()))


def densify_kernel(n_rows, rows_in, cols_in, count, values, out, rows, cols, head, nxt, dups, sem, sems):
    slots = values.shape[0]
    places = out.shape[0] - slots
    zero = jnp.zeros((TILE, TILE), jnp.bfloat16)
    loads = [
        pltpu.make_async_copy(source, target, sems.at[i])
        for i, (source, target) in enumerate(
            ((rows_in, rows), (cols_in, cols))
        )
    ]
    for load in loads:
        load.start()

    def clear(p, _):
        head[p] = -1
        out[p] = zero
        return 0

    lax.fori_loop(0, places, clear, 0, unroll=8)
    for load in loads:
        load.wait()
    live = count[0, 0]

    def place(s, found):
        p = cols[0, 0, s] * n_rows + rows[0, 0, s]
        alive = s < live
        before = head[p]
        first = jnp.logical_and(alive, before < 0)
        again = jnp.logical_and(alive, before >= 0)
        head[p] = jnp.where(alive, s, before)
        nxt[s] = before
        dups[found] = p
        pltpu.make_async_copy(
            values.at[s], out.at[jnp.where(first, p, places + s)], sem
        ).start()
        return found + again.astype(jnp.int32)

    found = lax.fori_loop(0, slots, place, 0, unroll=8)
    pltpu.make_async_copy(values, out.at[pl.ds(places, slots)], sem).wait()

    def merge(i, _):
        p = dups[i]
        top = head[p]

        @pl.when(top >= 0)
        def _():
            head[p] = -1

            def more(state):
                return nxt[state[0]] >= 0

            def add(state):
                s, total = state
                return nxt[s], total + out[places + s].astype(jnp.float32)

            _, total = lax.while_loop(more, add, (top, out[p].astype(jnp.float32)))
            out[p] = total.astype(jnp.bfloat16)

        return 0

    lax.fori_loop(0, found, merge, 0)


def densify(rows, cols, count, values, n_rows, n_cols):
    slots = values.shape[0]
    places = n_rows * n_cols
    hbm = pl.BlockSpec(memory_space=pltpu.HBM)
    return pl.pallas_call(
        lambda *refs: densify_kernel(n_rows, *refs),
        out_shape=pltpu.VMEM((places + slots, TILE, TILE), jnp.bfloat16),
        in_specs=[hbm, hbm, pl.BlockSpec(memory_space=pltpu.SMEM), hbm],
        out_specs=pl.BlockSpec(memory_space=pltpu.VMEM),
        scratch_shapes=[
            pltpu.SMEM(rows.shape, jnp.int32),
            pltpu.SMEM(cols.shape, jnp.int32),
            pltpu.SMEM((places,), jnp.int32),
            pltpu.SMEM((slots,), jnp.int32),
            pltpu.SMEM((slots + 1,), jnp.int32),
            pltpu.SemaphoreType.DMA,
            pltpu.SemaphoreType.DMA((2,)),
        ],
        compiler_params=pltpu.CompilerParams(vmem_limit_bytes=4 * 2**20),
        name="densify",
    )(
        pltpu.with_memory_space_constraint(rows, pltpu.HBM),
        pltpu.with_memory_space_constraint(cols, pltpu.HBM),
        count,
        pltpu.with_memory_space_constraint(values, pltpu.HBM),
    )


class Exchange:
    def __init__(self, axis, size, dst, send_sem, recv_sem):
        self.axis, self.size, self.dst = axis, size, dst
        self.send_sem, self.recv_sem = send_sem, recv_sem
        self.me = lax.axis_index(axis)

    def copy(self, source, target, peer):
        return pltpu.make_async_remote_copy(
            src_ref=source,
            dst_ref=target,
            send_sem=self.send_sem,
            recv_sem=self.recv_sem,
            device_id={self.axis: peer},
            device_id_type=MESH,
        )

    def peers(self, body):
        def step(d, _):
            body(lax.rem(self.me + d, self.size))
            return 0

        lax.fori_loop(1, self.size, step, 0)

    def send(self, source, peer):
        self.copy(source, self.dst.at[self.me], peer).start()

    def send_all(self, source_of):
        self.peers(lambda peer: self.send(source_of(peer), peer))

    def everything(self):
        span = self.dst.at[pl.ds(0, self.size - 1)]
        return self.copy(span, span, lax.rem(self.me + 1, self.size))

    def receive_all(self):
        self.everything().wait_recv()

    def sent_all(self):
        self.everything().wait_send()


class Gather(Exchange):
    def copy(self, source, target, peer, slot=None):
        return pltpu.make_async_remote_copy(
            src_ref=source,
            dst_ref=target,
            send_sem=self.send_sem,
            recv_sem=self.recv_sem.at[self.me if slot is None else slot],
            device_id={self.axis: peer},
            device_id_type=MESH,
        )

    def receive(self, slot):
        self.copy(self.dst.at[slot], self.dst.at[slot], slot, slot).wait_recv()


def rows_of(dense, i, n_rows, n_cols):
    return jnp.concatenate(
        [dense[pl.ds(k * n_rows + 2 * i, 2)].reshape(2 * TILE, TILE) for k in range(n_cols)],
        axis=1,
    )


def cols_of(dense, k, n_rows):
    return jnp.concatenate(
        [
            dense[pl.ds((2 * k + h) * n_rows, n_rows)].reshape(n_rows * TILE, TILE)
            for h in range(2)
        ],
        axis=1,
    )


def add_up(ref, size):
    return lax.fori_loop(
        1, size, lambda j, total: total + ref[j].astype(jnp.float32), ref[0].astype(jnp.float32)
    )


def step_kernel(
    R,
    C,
    x,
    dense,
    labels,
    mask,
    w1,
    b1,
    w2,
    b2,
    hidden_out,
    logits_out,
    sums_out,
    xg,
    t1,
    r1,
    s2,
    hw,
    t2,
    r2,
    s3,
    gg,
    t3,
    r3,
    part,
    part16,
    r4,
    s5,
    r5,
    fin,
    first_acc,
    second_acc,
    back_acc,
    pre,
    agg,
    w2s,
    b2s,
    send_sems,
    x_sems,
    hw_sems,
    grad_sems,
    recv_sems,
):
    n_rows, n_cols = 2 * C, 2 * R
    nodes = x.shape[0]
    classes = w2.shape[0]
    piece = fin.shape[1]
    row, col = lax.axis_index("row"), lax.axis_index("col")

    barrier = pltpu.get_barrier_semaphore()

    def greet(axis, me, size):
        def one(d, _):
            pl.semaphore_signal(
                barrier,
                inc=1,
                device_id={axis: lax.rem(me + d, size)},
                device_id_type=MESH,
            )
            return 0

        lax.fori_loop(1, size, one, 0)

    greet("row", row, R)
    greet("col", col, C)

    ex_x = Gather("row", R, xg, send_sems.at[0], x_sems)
    ex_first = Exchange("col", C, r1, send_sems.at[1], recv_sems.at[1])
    ex_hw = Gather("row", R, hw, send_sems.at[2], hw_sems)
    ex_second = Exchange("col", C, r2, send_sems.at[3], recv_sems.at[3])
    ex_grad = Gather("col", C, gg, send_sems.at[4], grad_sems)
    ex_back = Exchange("row", R, r3, send_sems.at[5], recv_sems.at[5])
    ex_part = Exchange("col", C, r4, send_sems.at[6], recv_sems.at[6])
    ex_sum = Exchange("row", R, r5, send_sems.at[7], recv_sems.at[7])
    ex_fin = Exchange("col", C, fin, send_sems.at[8], recv_sems.at[8])

    xg[row] = x[...]
    w2s[...] = jnp.zeros_like(w2s)
    w2s[0:classes, :] = w2[...].astype(jnp.float32)
    b2s[...] = jnp.zeros_like(b2s)
    b2s[0:1, 0:classes] = b2[...]
    first_acc[...] = jnp.zeros_like(first_acc)
    second_acc[...] = jnp.zeros_like(second_acc)
    back_acc[...] = jnp.zeros_like(back_acc)
    pl.semaphore_wait(barrier, R + C - 2)

    core = lax.rem(row, 2)
    beside = row + 1 - 2 * core

    def send_x(d, _):
        ex_x.send(x, lax.rem(row + 2 * d, R))
        return 0

    lax.fori_loop(1, R // 2, send_x, 0)
    ex_x.send(x, beside)

    def use_x(slot):
        first_acc[...] += jnp.dot(
            cols_of(dense, slot, n_rows), xg[slot], preferred_element_type=jnp.float32
        )

    use_x(row)
    ex_x.receive(beside)
    use_x(beside)

    def pass_x(d, _):
        slot = lax.rem(row + R - 2 * d, R)
        ex_x.receive(slot)
        ex_x.copy(xg.at[slot], xg.at[slot], beside, slot).start()
        use_x(slot)
        other = lax.rem(beside + R - 2 * d, R)
        ex_x.receive(other)
        use_x(other)
        return 0

    lax.fori_loop(1, R // 2, pass_x, 0)

    def first(d, _):
        peer = lax.rem(col + d, C)
        t1[peer] = first_acc[pl.ds(peer * nodes, nodes), :].astype(t1.dtype)

        @pl.when(d < C)
        def _():
            ex_first.send(t1.at[peer], peer)

        return 0

    lax.fori_loop(1, C + 1, first, 0)
    r1[col] = t1[col]
    ex_first.receive_all()

    agg[...] = add_up(r1, C).astype(jnp.bfloat16)
    v = jnp.dot(agg[...], w1[...], preferred_element_type=jnp.float32) + b1[...]
    pre[...] = v
    hidden_out[...] = (v / (1.0 + jnp.exp(-v))).astype(jnp.bfloat16)
    s2[...] = lax.dot_general(
        w2s[...].astype(jnp.bfloat16), hidden_out[...], NT, preferred_element_type=jnp.float32
    ).astype(jnp.bfloat16)

    hw[row] = s2[...]
    ex_hw.send_all(lambda peer: s2)

    def use_hw(d, _):
        slot = lax.rem(row + R - d, R)

        @pl.when(d > 0)
        def _():
            ex_hw.receive(slot)

        second_acc[...] += lax.dot_general(
            hw[slot], cols_of(dense, slot, n_rows), NT, preferred_element_type=jnp.float32
        )
        return 0

    lax.fori_loop(0, R, use_hw, 0)

    def second(d, _):
        peer = lax.rem(col + d, C)
        t2[peer] = second_acc[:, pl.ds(pl.multiple_of(peer * nodes, nodes), nodes)].astype(t2.dtype)

        @pl.when(d < C)
        def _():
            ex_second.send(t2.at[peer], peer)

        return 0

    lax.fori_loop(1, C + 1, second, 0)
    r2[col] = t2[col]
    ex_second.receive_all()

    turned = jnp.transpose(jnp.broadcast_to(b2s[0:1, :], (TILE, TILE)))[0:PADDED, :]
    logits = add_up(r2, C) + jnp.concatenate([turned] * (nodes // TILE), axis=1)
    logits_out[...] = logits[0:classes, :]
    index = lax.broadcasted_iota(jnp.int32, (PADDED, nodes), 0)
    real = index < classes
    top = jnp.max(jnp.where(real, logits, -jnp.inf), axis=0, keepdims=True)
    terms = jnp.where(real, jnp.exp(logits - top), 0.0)
    log_total = top + jnp.log(jnp.sum(terms, axis=0, keepdims=True))
    onehot = (index == labels[...]).astype(jnp.float32)
    weights = mask[...].astype(jnp.float32)
    cross = weights * (log_total - jnp.sum(onehot * logits, axis=0, keepdims=True))
    grad = jnp.where(real, jnp.exp(logits - log_total) - onehot, 0.0) * weights
    s3[...] = grad.astype(jnp.bfloat16)

    gg[col] = s3[...]
    ex_grad.send_all(lambda peer: s3)

    def halves(base, value):
        height = value.shape[0]
        for h in range(2):
            part[pl.ds(base + h * height, height), :] = value[:, h * TILE : (h + 1) * TILE]

    base2, base3 = 2 * w1.shape[0], 2 * w1.shape[0] + 2 * PADDED
    ones = jnp.ones((8, nodes), jnp.float32)
    b2_part = lax.dot_general(
        ones, grad, NT, precision=lax.Precision.HIGHEST, preferred_element_type=jnp.float32
    )
    part[pl.ds(base3, 32), :] = jnp.zeros((32, TILE), jnp.float32)
    part[pl.ds(base3 + 2, 1), 0:PADDED] = b2_part[0:1, :]
    part[pl.ds(base3 + 3, 1), :] = jnp.broadcast_to(
        jnp.sum(cross, axis=1, keepdims=True), (1, TILE)
    )
    part[pl.ds(base3 + 4, 1), :] = jnp.broadcast_to(
        jnp.sum(weights, axis=1, keepdims=True), (1, TILE)
    )

    def use_grad(d, _):
        slot = lax.rem(col + C - d, C)

        @pl.when(d > 0)
        def _():
            ex_grad.receive(slot)

        back_acc[...] += jnp.dot(
            gg[slot], rows_of(dense, slot, n_rows, n_cols), preferred_element_type=jnp.float32
        )
        return 0

    lax.fori_loop(0, C, use_grad, 0)

    def back(d, _):
        peer = lax.rem(row + d, R)
        t3[peer] = back_acc[:, pl.ds(pl.multiple_of(peer * nodes, nodes), nodes)].astype(t3.dtype)

        @pl.when(d < R)
        def _():
            ex_back.send(t3.at[peer], peer)

        return 0

    lax.fori_loop(1, R + 1, back, 0)
    r3[row] = t3[row]
    ex_back.receive_all()

    turned_grad = add_up(r3, R).astype(jnp.bfloat16)
    hidden_grad = lax.dot_general(
        turned_grad, w2s[...].astype(jnp.bfloat16), TN, preferred_element_type=jnp.float32
    )
    v = pre[...]
    s = 1.0 / (1.0 + jnp.exp(-v))
    pre_grad = hidden_grad * s * (1.0 + v * (1.0 - s))
    b1_part = jnp.sum(pre_grad, axis=0, keepdims=True)
    for h in range(2):
        part[pl.ds(base3 + h, 1), :] = b1_part[:, h * TILE : (h + 1) * TILE]
    halves(
        0,
        lax.dot_general(
            agg[...], pre_grad.astype(jnp.bfloat16), TN, preferred_element_type=jnp.float32
        ),
    )
    halves(
        base2,
        jnp.dot(turned_grad, hidden_out[...], preferred_element_type=jnp.float32),
    )

    def split(value):
        high = value.astype(jnp.bfloat16)
        return high, (value - high.astype(jnp.float32)).astype(jnp.bfloat16)

    last = C - 1
    part16[pl.ds(0, base3), :] = part[pl.ds(0, base3), :].astype(jnp.bfloat16)
    high, low = split(part[pl.ds(base3, 16), :])
    part16[pl.ds(base3, 16), :] = high
    part16[pl.ds(base3 + 16, 16), :] = low
    ex_part.send_all(
        lambda peer: part16.at[pl.ds(pl.multiple_of(peer * piece, piece), piece)]
    )
    r4[col] = part16[pl.ds(pl.multiple_of(col * piece, piece), piece), :]
    ex_part.receive_all()

    def resplit(total):
        high, low = split(total[piece - 32 : piece - 16, :] + total[piece - 16 :, :])
        both = jnp.concatenate([high, low], axis=0)
        plain = total.astype(jnp.bfloat16)
        tail = jnp.where(col == last, both, plain[piece - 32 :, :])
        return jnp.concatenate([plain[: piece - 32, :], tail], axis=0)

    s5[...] = resplit(add_up(r4, C))
    r5[row] = s5[...]
    ex_sum.send_all(lambda peer: s5)
    ex_sum.receive_all()

    fin[col] = resplit(add_up(r5, R))
    ex_fin.send_all(lambda peer: fin.at[col])
    ex_fin.receive_all()

    for j in range(C):
        sums_out[j * piece : (j + 1) * piece, :] = fin[j].astype(jnp.float32)
    for ex in (ex_first, ex_hw, ex_second, ex_grad, ex_back, ex_part, ex_sum, ex_fin):
        ex.sent_all()
    ex_x.sent_all()


def finish_kernel(
    features,
    classes,
    hidden,
    logits,
    sums,
    hidden_out,
    logits_out,
    loss_out,
    w1_grad_out,
    b1_grad_out,
    w2_grad_out,
    b2_grad_out,
    sems,
):
    copies = [
        pltpu.make_async_copy(hidden, hidden_out, sems.at[0]),
        pltpu.make_async_copy(logits, logits_out, sems.at[1]),
    ]
    for copy in copies:
        copy.start()
    base2, base3 = 2 * features, 2 * features + 2 * PADDED
    small = sums[base3 : base3 + 16, :] + sums[base3 + 16 : base3 + 32, :]
    count = small[4:5, 0:1]
    for h in range(2):
        lanes = slice(h * TILE, (h + 1) * TILE)
        w1_grad_out[:, lanes] = sums[h * features : (h + 1) * features, :] / count
        low = base2 + h * PADDED
        w2_grad_out[:, lanes] = sums[low : low + classes, :] / count
        b1_grad_out[:, lanes] = small[h : h + 1, :] / count
    b2_grad_out[...] = small[2:3, 0:classes] / count
    loss_out[...] = small[3:4, 0:1] / count
    for copy in copies:
        copy.wait()


def on_device(
    node_features,
    tile_values,
    tile_rows,
    tile_cols,
    tile_count,
    labels,
    train_mask,
    hidden_weight,
    hidden_bias,
    class_weight,
    class_bias,
):
    nodes, features = node_features.shape
    hidden, classes = class_weight.shape
    R, C = lax.axis_size("row"), lax.axis_size("col")
    n_rows, n_cols = C * nodes // TILE, R * nodes // TILE
    dense = densify(tile_rows, tile_cols, tile_count, tile_values[0, 0], n_rows, n_cols)
    used = 2 * features + 2 * PADDED + 32
    piece = used // C
    vmem = pl.BlockSpec(memory_space=pltpu.VMEM)
    hbm = pl.BlockSpec(memory_space=pltpu.HBM)
    bf16, f32 = jnp.bfloat16, jnp.float32
    out = lambda shape, kind: jax.ShapeDtypeStruct(shape, kind)
    scratch = [
        pltpu.VMEM((R, nodes, features), bf16),
        pltpu.VMEM((C, nodes, features), bf16),
        pltpu.VMEM((C, nodes, features), bf16),
        pltpu.VMEM((PADDED, nodes), bf16),
        pltpu.VMEM((R, PADDED, nodes), bf16),
        pltpu.VMEM((C, PADDED, nodes), bf16),
        pltpu.VMEM((C, PADDED, nodes), bf16),
        pltpu.VMEM((PADDED, nodes), bf16),
        pltpu.VMEM((C, PADDED, nodes), bf16),
        pltpu.VMEM((R, PADDED, nodes), bf16),
        pltpu.VMEM((R, PADDED, nodes), bf16),
        pltpu.VMEM((used, TILE), f32),
        pltpu.VMEM((used, TILE), bf16),
        pltpu.VMEM((C, piece, TILE), bf16),
        pltpu.VMEM((piece, TILE), bf16),
        pltpu.VMEM((R, piece, TILE), bf16),
        pltpu.VMEM((C, piece, TILE), bf16),
        pltpu.VMEM((C * nodes, features), f32),
        pltpu.VMEM((PADDED, C * nodes), f32),
        pltpu.VMEM((PADDED, R * nodes), f32),
        pltpu.VMEM((nodes, hidden), f32),
        pltpu.VMEM((nodes, features), bf16),
        pltpu.VMEM((PADDED, hidden), f32),
        pltpu.VMEM((8, TILE), f32),
        pltpu.SemaphoreType.DMA((9,)),
        pltpu.SemaphoreType.DMA((R,)),
        pltpu.SemaphoreType.DMA((R,)),
        pltpu.SemaphoreType.DMA((C,)),
        pltpu.SemaphoreType.DMA((9,)),
    ]
    hidden_now, logits_now, sums = pl.pallas_call(
        lambda *refs: step_kernel(R, C, *refs),
        out_shape=(
            pltpu.VMEM((nodes, hidden), bf16),
            pltpu.VMEM((classes, nodes), f32),
            pltpu.VMEM((used, TILE), f32),
        ),
        in_specs=[vmem] * 8,
        out_specs=(vmem,) * 3,
        scratch_shapes=scratch,
        compiler_params=pltpu.CompilerParams(
            collective_id=0, has_side_effects=True, vmem_limit_bytes=24 * 2**20
        ),
        name="step",
    )(
        node_features,
        pltpu.with_memory_space_constraint(dense, pltpu.VMEM),
        labels.reshape(1, nodes),
        train_mask.reshape(1, nodes),
        hidden_weight,
        hidden_bias.reshape(1, hidden),
        class_weight.T,
        class_bias.reshape(1, classes),
    )
    hidden_out, logits, loss, w1_grad, b1_grad, w2_grad, b2_grad = pl.pallas_call(
        lambda *refs: finish_kernel(features, classes, *refs),
        out_shape=(
            out((nodes, hidden), bf16),
            out((classes, nodes), f32),
            out((1, 1), f32),
            out((features, hidden), f32),
            out((1, hidden), f32),
            out((classes, hidden), f32),
            out((1, classes), f32),
        ),
        in_specs=[vmem] * 3,
        out_specs=(hbm, hbm) + (vmem,) * 5,
        scratch_shapes=[pltpu.SemaphoreType.DMA((2,))],
        compiler_params=pltpu.CompilerParams(vmem_limit_bytes=4 * 2**20),
        name="finish",
    )(*(pltpu.with_memory_space_constraint(a, pltpu.VMEM) for a in (hidden_now, logits_now, sums)))
    return (
        hidden_out,
        logits,
        loss[0, 0],
        w1_grad,
        b1_grad[0],
        w2_grad.T,
        b2_grad[0],
    )


def solution(mesh):
    in_specs = (
        P(("row", "col"), None),
        P("row", "col", None, None, None),
        P("row", "col", None),
        P("row", "col", None),
        P("row", "col"),
        P(("row", "col")),
        P(("row", "col")),
        P(),
        P(),
        P(),
        P(),
    )
    out_specs = (P(("row", "col"), None), P(None, ("row", "col")), P(), P(), P(), P(), P())
    return jax.shard_map(
        on_device, mesh=mesh, in_specs=in_specs, out_specs=out_specs, check_vma=False
    )
```

```python
import jax
import jax.numpy as jnp
from jax import lax
from jax.experimental import pallas as pl
from jax.experimental.pallas import tpu as pltpu
from jax.sharding import PartitionSpec as P

TILE = 128
PADDED = 48
MESH = pl.DeviceIdType.MESH
NT = (((1,), (1,)), ((), ()))
TN = (((0,), (0,)), ((), ()))


def densify_kernel(n_rows, rows_in, cols_in, count, values, out, rows, cols, head, nxt, pairs, longer, sem, sems):
    slots = values.shape[0]
    places = head.shape[0]
    spare = places + slots
    zero = jnp.zeros((TILE, TILE), jnp.bfloat16)
    loads = [
        pltpu.make_async_copy(source, target, sems.at[i])
        for i, (source, target) in enumerate(
            ((rows_in, rows), (cols_in, cols))
        )
    ]
    for load in loads:
        load.start()

    def clear(p, _):
        head[p] = -1
        return 0

    lax.fori_loop(0, places, clear, 0, unroll=8)
    for load in loads:
        load.wait()
    live = count[0, 0]

    def place(s, found):
        seconds, more = found
        p = cols[0, 0, s] * n_rows + rows[0, 0, s]
        alive = s < live
        before = head[p]
        vacant = before < 0
        below = nxt[jnp.maximum(before, 0)]
        first = jnp.logical_and(alive, vacant)
        again = jnp.logical_and(alive, jnp.logical_not(vacant))
        head[p] = jnp.where(alive, s, before)
        nxt[s] = before
        pairs[seconds] = p * slots + s
        longer[more] = p
        pltpu.make_async_copy(
            values.at[s], out.at[jnp.where(first, p, places + s)], sem
        ).start()
        second = jnp.logical_and(again, below < 0)
        third = jnp.logical_and(again, below >= 0)
        return seconds + second.astype(jnp.int32), more + third.astype(jnp.int32)

    seconds, more = lax.fori_loop(0, slots, place, (0, 0), unroll=8)

    def blank(p, _):
        out[jnp.where(head[p] < 0, p, spare)] = zero
        return 0

    lax.fori_loop(0, places, blank, 0, unroll=8)
    pltpu.make_async_copy(values, out.at[pl.ds(places, slots)], sem).wait()

    def merge(i, _):
        p = longer[i]
        top = head[p]

        @pl.when(top >= 0)
        def _():
            head[p] = -1

            def going(state):
                return nxt[state[0]] >= 0

            def add(state):
                s, total = state
                tile = out[places + s].astype(jnp.float32)
                out[places + s] = zero
                return nxt[s], total + tile

            _, total = lax.while_loop(going, add, (top, out[p].astype(jnp.float32)))
            out[p] = total.astype(jnp.bfloat16)

        return 0

    lax.fori_loop(0, more, merge, 0)

    def add_second(i, _):
        p = pairs[i] // slots
        s = pairs[i] - p * slots
        both = out[p].astype(jnp.float32) + out[places + s].astype(jnp.float32)
        out[p] = both.astype(jnp.bfloat16)
        return 0

    lax.fori_loop(0, seconds, add_second, 0)


def densify(rows, cols, count, values, n_rows, n_cols):
    slots = values.shape[0]
    places = n_rows * n_cols
    hbm = pl.BlockSpec(memory_space=pltpu.HBM)
    return pl.pallas_call(
        lambda *refs: densify_kernel(n_rows, *refs),
        out_shape=pltpu.VMEM((places + slots + 1, TILE, TILE), jnp.bfloat16),
        in_specs=[hbm, hbm, pl.BlockSpec(memory_space=pltpu.SMEM), hbm],
        out_specs=pl.BlockSpec(memory_space=pltpu.VMEM),
        scratch_shapes=[
            pltpu.SMEM(rows.shape, jnp.int32),
            pltpu.SMEM(cols.shape, jnp.int32),
            pltpu.SMEM((places,), jnp.int32),
            pltpu.SMEM((slots,), jnp.int32),
            pltpu.SMEM((slots + 1,), jnp.int32),
            pltpu.SMEM((slots + 1,), jnp.int32),
            pltpu.SemaphoreType.DMA,
            pltpu.SemaphoreType.DMA((2,)),
        ],
        compiler_params=pltpu.CompilerParams(vmem_limit_bytes=4 * 2**20),
        name="densify",
    )(
        pltpu.with_memory_space_constraint(rows, pltpu.HBM),
        pltpu.with_memory_space_constraint(cols, pltpu.HBM),
        count,
        pltpu.with_memory_space_constraint(values, pltpu.HBM),
    )


class Exchange:
    def __init__(self, axis, size, dst, send_sem, recv_sem):
        self.axis, self.size, self.dst = axis, size, dst
        self.send_sem, self.recv_sem = send_sem, recv_sem
        self.me = lax.axis_index(axis)

    def copy(self, source, target, peer):
        return pltpu.make_async_remote_copy(
            src_ref=source,
            dst_ref=target,
            send_sem=self.send_sem,
            recv_sem=self.recv_sem,
            device_id={self.axis: peer},
            device_id_type=MESH,
        )

    def peer(self, d):
        me, size = self.me, self.size
        if self.axis == "col":
            half = size // 2
            step = lax.rem(1 + d, half)
            return lax.rem(me // half + 1 - d // half, 2) * half + lax.rem(me + step, half)
        q = self.chip(lax.div(d, 2), 1)
        return 2 * q + lax.rem(me + 1 + d, 2)

    def chip(self, d, sign):
        q, half = self.me // 2, self.size // 4
        step = lax.rem(1 + d, half)
        return lax.rem(q // half + 1 - d // half, 2) * half + lax.rem(q + half + sign * step, half)

    def peers(self, body):
        def step(d, _):
            body(self.peer(d))
            return 0

        lax.fori_loop(0, self.size - 1, step, 0)

    def send(self, source, peer):
        self.copy(source, self.dst.at[self.me], peer).start()

    def send_all(self, source_of):
        self.peers(lambda peer: self.send(source_of(peer), peer))

    def everything(self):
        span = self.dst.at[pl.ds(0, self.size - 1)]
        return self.copy(span, span, lax.rem(self.me + 1, self.size))

    def receive_all(self):
        self.everything().wait_recv()

    def sent_all(self):
        self.everything().wait_send()


class Gather(Exchange):
    def copy(self, source, target, peer, slot=None):
        return pltpu.make_async_remote_copy(
            src_ref=source,
            dst_ref=target,
            send_sem=self.send_sem,
            recv_sem=self.recv_sem.at[self.me if slot is None else slot],
            device_id={self.axis: peer},
            device_id_type=MESH,
        )

    def receive(self, slot):
        self.copy(self.dst.at[slot], self.dst.at[slot], slot, slot).wait_recv()

    def by_chip(self, source, use):
        me, chips = self.me, self.size // 2
        own, core = me // 2, lax.rem(me, 2)
        beside = 2 * own + 1 - core

        def send(d, _):
            self.send(source, 2 * self.chip(d, 1) + core)
            return 0

        self.send(source, beside)
        lax.fori_loop(0, chips - 1, send, 0)
        self.receive(beside)
        use(own)

        def take(q):
            slot = 2 * q + core
            self.receive(slot)
            self.copy(self.dst.at[slot], self.dst.at[slot], beside, slot).start()

        def turn(q):
            self.receive(2 * q + 1 - core)
            use(q)

        take(self.chip(chips - 2, -1))

        def step(e, _):
            take(self.chip(chips - 2 - e, -1))
            turn(self.chip(chips - 1 - e, -1))
            return 0

        lax.fori_loop(1, chips - 1, step, 0)
        turn(self.chip(0, -1))


def rows_of(dense, i, n_rows, n_cols):
    return jnp.concatenate(
        [dense[pl.ds(k * n_rows + 2 * i, 2)].reshape(2 * TILE, TILE) for k in range(n_cols)],
        axis=1,
    )


def cols_of(dense, q, n_rows):
    return jnp.concatenate(
        [
            dense[pl.ds((4 * q + h) * n_rows, n_rows)].reshape(n_rows * TILE, TILE)
            for h in range(4)
        ],
        axis=1,
    )


def add_up(ref, size):
    return lax.fori_loop(
        1, size, lambda j, total: total + ref[j].astype(jnp.float32), ref[0].astype(jnp.float32)
    )


def step_kernel(
    R,
    C,
    x,
    dense,
    labels,
    mask,
    w1,
    b1,
    w2,
    b2,
    hidden_out,
    logits_out,
    sums_out,
    xg,
    t1,
    r1,
    s2,
    hw,
    t2,
    r2,
    s3,
    gg,
    t3,
    r3,
    part,
    part16,
    r4,
    s5,
    r5,
    fin,
    first_acc,
    second_acc,
    pre,
    agg,
    w2s,
    b2s,
    send_sems,
    x_sems,
    hw_sems,
    recv_sems,
):
    n_rows, n_cols = 2 * C, 2 * R
    nodes = x.shape[0]
    classes = w2.shape[0]
    piece = fin.shape[1]
    row, col = lax.axis_index("row"), lax.axis_index("col")

    barrier = pltpu.get_barrier_semaphore()

    def greet(axis, me, size):
        def one(d, _):
            pl.semaphore_signal(
                barrier,
                inc=1,
                device_id={axis: lax.rem(me + d, size)},
                device_id_type=MESH,
            )
            return 0

        lax.fori_loop(1, size, one, 0)

    greet("row", row, R)
    greet("col", col, C)

    ex_x = Gather("row", R, xg, send_sems.at[0], x_sems)
    ex_first = Exchange("col", C, r1, send_sems.at[1], recv_sems.at[1])
    ex_hw = Gather("row", R, hw, send_sems.at[2], hw_sems)
    ex_second = Exchange("col", C, r2, send_sems.at[3], recv_sems.at[3])
    ex_grad = Exchange("col", C, gg, send_sems.at[4], recv_sems.at[4])
    ex_back = Exchange("row", R, r3, send_sems.at[5], recv_sems.at[5])
    ex_part = Exchange("col", C, r4, send_sems.at[6], recv_sems.at[6])
    ex_sum = Exchange("row", R, r5, send_sems.at[7], recv_sems.at[7])
    ex_fin = Exchange("col", C, fin, send_sems.at[8], recv_sems.at[8])

    xg[row] = x[...]
    w2s[...] = jnp.zeros_like(w2s)
    w2s[0:classes, :] = w2[...].astype(jnp.float32)
    b2s[...] = jnp.zeros_like(b2s)
    b2s[0:1, 0:classes] = b2[...]
    first_acc[...] = jnp.zeros_like(first_acc)
    second_acc[...] = jnp.zeros_like(second_acc)
    pl.semaphore_wait(barrier, R + C - 2)

    def use_x(q):
        first_acc[...] += jnp.dot(
            cols_of(dense, q, n_rows),
            xg[pl.ds(2 * q, 2)].reshape(2 * nodes, x.shape[1]),
            preferred_element_type=jnp.float32,
        )

    ex_x.by_chip(x, use_x)

    def first(d, _):
        peer = ex_first.peer(d)
        t1[peer] = first_acc[pl.ds(peer * nodes, nodes), :].astype(t1.dtype)

        @pl.when(d < C - 1)
        def _():
            ex_first.send(t1.at[peer], peer)

        return 0

    lax.fori_loop(0, C, first, 0)
    r1[col] = t1[col]
    ex_first.receive_all()

    agg[...] = add_up(r1, C).astype(jnp.bfloat16)
    v = jnp.dot(agg[...], w1[...], preferred_element_type=jnp.float32) + b1[...]
    pre[...] = v
    hidden_out[...] = (v / (1.0 + jnp.exp(-v))).astype(jnp.bfloat16)
    s2[...] = lax.dot_general(
        w2s[...].astype(jnp.bfloat16), hidden_out[...], NT, preferred_element_type=jnp.float32
    ).astype(jnp.bfloat16)

    hw[row] = s2[...]
    def use_hw(q):
        second_acc[...] += lax.dot_general(
            jnp.concatenate([hw[2 * q], hw[2 * q + 1]], axis=1),
            cols_of(dense, q, n_rows),
            NT,
            preferred_element_type=jnp.float32,
        )

    ex_hw.by_chip(s2, use_hw)

    def second(d, _):
        peer = ex_second.peer(d)
        t2[peer] = second_acc[:, pl.ds(pl.multiple_of(peer * nodes, nodes), nodes)].astype(t2.dtype)

        @pl.when(d < C - 1)
        def _():
            ex_second.send(t2.at[peer], peer)

        return 0

    lax.fori_loop(0, C, second, 0)
    r2[col] = t2[col]
    ex_second.receive_all()

    turned = jnp.transpose(jnp.broadcast_to(b2s[0:1, :], (TILE, TILE)))[0:PADDED, :]
    logits = add_up(r2, C) + jnp.concatenate([turned] * (nodes // TILE), axis=1)
    logits_out[...] = logits[0:classes, :]
    index = lax.broadcasted_iota(jnp.int32, (PADDED, nodes), 0)
    real = index < classes
    top = jnp.max(jnp.where(real, logits, -jnp.inf), axis=0, keepdims=True)
    terms = jnp.where(real, jnp.exp(logits - top), 0.0)
    log_total = top + jnp.log(jnp.sum(terms, axis=0, keepdims=True))
    onehot = (index == labels[...]).astype(jnp.float32)
    weights = mask[...].astype(jnp.float32)
    cross = weights * (log_total - jnp.sum(onehot * logits, axis=0, keepdims=True))
    grad = jnp.where(real, jnp.exp(logits - log_total) - onehot, 0.0) * weights
    s3[...] = grad.astype(jnp.bfloat16)

    gg[col] = s3[...]
    ex_grad.send_all(lambda peer: s3)

    def halves(base, value):
        height = value.shape[0]
        for h in range(2):
            part[pl.ds(base + h * height, height), :] = value[:, h * TILE : (h + 1) * TILE]

    base2, base3 = 2 * w1.shape[0], 2 * w1.shape[0] + 2 * PADDED
    ones = jnp.ones((8, nodes), jnp.float32)
    b2_part = lax.dot_general(
        ones, grad, NT, precision=lax.Precision.HIGHEST, preferred_element_type=jnp.float32
    )
    part[pl.ds(base3, 32), :] = jnp.zeros((32, TILE), jnp.float32)
    part[pl.ds(base3 + 2, 1), 0:PADDED] = b2_part[0:1, :]
    part[pl.ds(base3 + 3, 1), :] = jnp.broadcast_to(
        jnp.sum(cross, axis=1, keepdims=True), (1, TILE)
    )
    part[pl.ds(base3 + 4, 1), :] = jnp.broadcast_to(
        jnp.sum(weights, axis=1, keepdims=True), (1, TILE)
    )

    ex_grad.receive_all()

    def back(d, _):
        q = ex_back.chip(d, 1)
        left = jnp.concatenate([gg[k] for k in range(C)], axis=1)
        both = jnp.dot(left, cols_of(dense, q, n_rows), preferred_element_type=jnp.float32)
        for h in range(2):
            t3[2 * q + h] = both[:, h * nodes : (h + 1) * nodes].astype(t3.dtype)

        @pl.when(d < R // 2 - 1)
        def _():
            for h in range(2):
                ex_back.send(t3.at[2 * q + h], 2 * q + h)

        return 0

    lax.fori_loop(0, R // 2, back, 0)
    beside = row + 1 - 2 * lax.rem(row, 2)
    ex_back.send(t3.at[beside], beside)
    r3[row] = t3[row]
    ex_back.receive_all()

    turned_grad = add_up(r3, R).astype(jnp.bfloat16)
    hidden_grad = lax.dot_general(
        turned_grad, w2s[...].astype(jnp.bfloat16), TN, preferred_element_type=jnp.float32
    )
    v = pre[...]
    s = 1.0 / (1.0 + jnp.exp(-v))
    pre_grad = hidden_grad * s * (1.0 + v * (1.0 - s))
    b1_part = jnp.sum(pre_grad, axis=0, keepdims=True)
    for h in range(2):
        part[pl.ds(base3 + h, 1), :] = b1_part[:, h * TILE : (h + 1) * TILE]
    halves(
        0,
        lax.dot_general(
            agg[...], pre_grad.astype(jnp.bfloat16), TN, preferred_element_type=jnp.float32
        ),
    )
    halves(
        base2,
        jnp.dot(turned_grad, hidden_out[...], preferred_element_type=jnp.float32),
    )

    def split(value):
        high = value.astype(jnp.bfloat16)
        return high, (value - high.astype(jnp.float32)).astype(jnp.bfloat16)

    last = C - 1
    part16[pl.ds(0, base3), :] = part[pl.ds(0, base3), :].astype(jnp.bfloat16)
    high, low = split(part[pl.ds(base3, 16), :])
    part16[pl.ds(base3, 16), :] = high
    part16[pl.ds(base3 + 16, 16), :] = low
    ex_part.send_all(
        lambda peer: part16.at[pl.ds(pl.multiple_of(peer * piece, piece), piece)]
    )
    r4[col] = part16[pl.ds(pl.multiple_of(col * piece, piece), piece), :]
    ex_part.receive_all()

    def resplit(total):
        high, low = split(total[piece - 32 : piece - 16, :] + total[piece - 16 :, :])
        both = jnp.concatenate([high, low], axis=0)
        plain = total.astype(jnp.bfloat16)
        tail = jnp.where(col == last, both, plain[piece - 32 :, :])
        return jnp.concatenate([plain[: piece - 32, :], tail], axis=0)

    s5[...] = resplit(add_up(r4, C))
    r5[row] = s5[...]
    ex_sum.send_all(lambda peer: s5)
    ex_sum.receive_all()

    fin[col] = resplit(add_up(r5, R))
    ex_fin.send_all(lambda peer: fin.at[col])
    ex_fin.receive_all()

    for j in range(C):
        sums_out[j * piece : (j + 1) * piece, :] = fin[j].astype(jnp.float32)
    for ex in (ex_first, ex_hw, ex_second, ex_grad, ex_back, ex_part, ex_sum, ex_fin):
        ex.sent_all()
    ex_x.sent_all()


def finish_kernel(
    features,
    classes,
    hidden,
    logits,
    sums,
    hidden_out,
    logits_out,
    loss_out,
    w1_grad_out,
    b1_grad_out,
    w2_grad_out,
    b2_grad_out,
    sems,
):
    copies = [
        pltpu.make_async_copy(hidden, hidden_out, sems.at[0]),
        pltpu.make_async_copy(logits, logits_out, sems.at[1]),
    ]
    for copy in copies:
        copy.start()
    base2, base3 = 2 * features, 2 * features + 2 * PADDED
    small = sums[base3 : base3 + 16, :] + sums[base3 + 16 : base3 + 32, :]
    count = small[4:5, 0:1]
    for h in range(2):
        lanes = slice(h * TILE, (h + 1) * TILE)
        w1_grad_out[:, lanes] = sums[h * features : (h + 1) * features, :] / count
        low = base2 + h * PADDED
        w2_grad_out[:, lanes] = sums[low : low + classes, :] / count
        b1_grad_out[:, lanes] = small[h : h + 1, :] / count
    b2_grad_out[...] = small[2:3, 0:classes] / count
    loss_out[...] = small[3:4, 0:1] / count
    for copy in copies:
        copy.wait()


def on_device(
    node_features,
    tile_values,
    tile_rows,
    tile_cols,
    tile_count,
    labels,
    train_mask,
    hidden_weight,
    hidden_bias,
    class_weight,
    class_bias,
):
    nodes, features = node_features.shape
    hidden, classes = class_weight.shape
    R, C = lax.axis_size("row"), lax.axis_size("col")
    n_rows, n_cols = C * nodes // TILE, R * nodes // TILE
    dense = densify(tile_rows, tile_cols, tile_count, tile_values[0, 0], n_rows, n_cols)
    used = 2 * features + 2 * PADDED + 32
    piece = used // C
    vmem = pl.BlockSpec(memory_space=pltpu.VMEM)
    hbm = pl.BlockSpec(memory_space=pltpu.HBM)
    bf16, f32 = jnp.bfloat16, jnp.float32
    out = lambda shape, kind: jax.ShapeDtypeStruct(shape, kind)
    scratch = [
        pltpu.VMEM((R, nodes, features), bf16),
        pltpu.VMEM((C, nodes, features), bf16),
        pltpu.VMEM((C, nodes, features), bf16),
        pltpu.VMEM((PADDED, nodes), bf16),
        pltpu.VMEM((R, PADDED, nodes), bf16),
        pltpu.VMEM((C, PADDED, nodes), bf16),
        pltpu.VMEM((C, PADDED, nodes), bf16),
        pltpu.VMEM((PADDED, nodes), bf16),
        pltpu.VMEM((C, PADDED, nodes), bf16),
        pltpu.VMEM((R, PADDED, nodes), bf16),
        pltpu.VMEM((R, PADDED, nodes), bf16),
        pltpu.VMEM((used, TILE), f32),
        pltpu.VMEM((used, TILE), bf16),
        pltpu.VMEM((C, piece, TILE), bf16),
        pltpu.VMEM((piece, TILE), bf16),
        pltpu.VMEM((R, piece, TILE), bf16),
        pltpu.VMEM((C, piece, TILE), bf16),
        pltpu.VMEM((C * nodes, features), f32),
        pltpu.VMEM((PADDED, C * nodes), f32),
        pltpu.VMEM((nodes, hidden), f32),
        pltpu.VMEM((nodes, features), bf16),
        pltpu.VMEM((PADDED, hidden), f32),
        pltpu.VMEM((8, TILE), f32),
        pltpu.SemaphoreType.DMA((9,)),
        pltpu.SemaphoreType.DMA((R,)),
        pltpu.SemaphoreType.DMA((R,)),
        pltpu.SemaphoreType.DMA((9,)),
    ]
    hidden_now, logits_now, sums = pl.pallas_call(
        lambda *refs: step_kernel(R, C, *refs),
        out_shape=(
            pltpu.VMEM((nodes, hidden), bf16),
            pltpu.VMEM((classes, nodes), f32),
            pltpu.VMEM((used, TILE), f32),
        ),
        in_specs=[vmem] * 8,
        out_specs=(vmem,) * 3,
        scratch_shapes=scratch,
        compiler_params=pltpu.CompilerParams(
            collective_id=0, has_side_effects=True, vmem_limit_bytes=24 * 2**20
        ),
        name="step",
    )(
        node_features,
        pltpu.with_memory_space_constraint(dense, pltpu.VMEM),
        labels.reshape(1, nodes),
        train_mask.reshape(1, nodes),
        hidden_weight,
        hidden_bias.reshape(1, hidden),
        class_weight.T,
        class_bias.reshape(1, classes),
    )
    hidden_out, logits, loss, w1_grad, b1_grad, w2_grad, b2_grad = pl.pallas_call(
        lambda *refs: finish_kernel(features, classes, *refs),
        out_shape=(
            out((nodes, hidden), bf16),
            out((classes, nodes), f32),
            out((1, 1), f32),
            out((features, hidden), f32),
            out((1, hidden), f32),
            out((classes, hidden), f32),
            out((1, classes), f32),
        ),
        in_specs=[vmem] * 3,
        out_specs=(hbm, hbm) + (vmem,) * 5,
        scratch_shapes=[pltpu.SemaphoreType.DMA((2,))],
        compiler_params=pltpu.CompilerParams(vmem_limit_bytes=4 * 2**20),
        name="finish",
    )(*(pltpu.with_memory_space_constraint(a, pltpu.VMEM) for a in (hidden_now, logits_now, sums)))
    return (
        hidden_out,
        logits,
        loss[0, 0],
        w1_grad,
        b1_grad[0],
        w2_grad.T,
        b2_grad[0],
    )


def solution(mesh):
    in_specs = (
        P(("row", "col"), None),
        P("row", "col", None, None, None),
        P("row", "col", None),
        P("row", "col", None),
        P("row", "col"),
        P(("row", "col")),
        P(("row", "col")),
        P(),
        P(),
        P(),
        P(),
    )
    out_specs = (P(("row", "col"), None), P(None, ("row", "col")), P(), P(), P(), P(), P())
    return jax.shard_map(
        on_device, mesh=mesh, in_specs=in_specs, out_specs=out_specs, check_vma=False
    )
```

```python
import jax
import jax.numpy as jnp
from jax import lax
from jax.experimental import pallas as pl
from jax.experimental.pallas import tpu as pltpu
from jax.sharding import PartitionSpec as P

TILE = 128
PADDED = 48
MESH = pl.DeviceIdType.MESH
NT = (((1,), (1,)), ((), ()))
TN = (((0,), (0,)), ((), ()))


def densify_kernel(n_rows, rows_in, cols_in, count, values, out, rows, cols, head, nxt, pairs, longer, sem, sems):
    slots = values.shape[0]
    places = head.shape[0]
    spare = places + slots
    several = 1 << (slots - 1).bit_length()
    zero = jnp.zeros((TILE, TILE), jnp.bfloat16)
    loads = [
        pltpu.make_async_copy(source, target, sems.at[i])
        for i, (source, target) in enumerate(
            ((rows_in, rows), (cols_in, cols))
        )
    ]
    for load in loads:
        load.start()

    def clear(p, _):
        head[p] = -1
        return 0

    lax.fori_loop(0, places, clear, 0, unroll=8)
    for load in loads:
        load.wait()
    live = count[0, 0]

    def place(s, found):
        seconds, more = found
        p = cols[0, 0, s] * n_rows + rows[0, 0, s]
        alive = s < live
        before = head[p]
        vacant = before < 0
        head[p] = jnp.where(alive, jnp.where(vacant, s, s + several), before)
        nxt[s] = before
        pairs[seconds] = p * several + s
        longer[more] = p
        pltpu.make_async_copy(
            values.at[s],
            out.at[jnp.where(jnp.logical_and(alive, vacant), p, places + s)],
            sem,
        ).start()
        third = jnp.logical_and(alive, before >= several)
        second = jnp.logical_and(alive, jnp.logical_and(before >= 0, before < several))
        return seconds + second.astype(jnp.int32), more + third.astype(jnp.int32)

    seconds, more = lax.fori_loop(0, slots, place, (0, 0), unroll=8)

    def slot_of(entry):
        return jnp.where(entry >= several, entry - several, entry)

    def blank(p, _):
        out[jnp.where(head[p] < 0, p, spare)] = zero
        return 0

    lax.fori_loop(0, places, blank, 0, unroll=8)
    pltpu.make_async_copy(values, out.at[pl.ds(places, slots)], sem).wait()

    def merge(i, _):
        p = longer[i]
        top = slot_of(head[p])

        @pl.when(top >= 0)
        def _():
            head[p] = -1

            def going(state):
                return nxt[state[0]] >= 0

            def add(state):
                s, total = state
                tile = out[places + s].astype(jnp.float32)
                out[places + s] = zero
                return slot_of(nxt[s]), total + tile

            _, total = lax.while_loop(going, add, (top, out[p].astype(jnp.float32)))
            out[p] = total.astype(jnp.bfloat16)

        return 0

    lax.fori_loop(0, more, merge, 0)

    def add_second(i, _):
        p = pairs[i] // several
        s = pairs[i] - p * several
        both = out[p].astype(jnp.float32) + out[places + s].astype(jnp.float32)
        out[p] = both.astype(jnp.bfloat16)
        return 0

    lax.fori_loop(0, seconds, add_second, 0)


def densify(rows, cols, count, values, n_rows, n_cols):
    slots = values.shape[0]
    places = n_rows * n_cols
    hbm = pl.BlockSpec(memory_space=pltpu.HBM)
    return pl.pallas_call(
        lambda *refs: densify_kernel(n_rows, *refs),
        out_shape=pltpu.VMEM((places + slots + 1, TILE, TILE), jnp.bfloat16),
        in_specs=[hbm, hbm, pl.BlockSpec(memory_space=pltpu.SMEM), hbm],
        out_specs=pl.BlockSpec(memory_space=pltpu.VMEM),
        scratch_shapes=[
            pltpu.SMEM(rows.shape, jnp.int32),
            pltpu.SMEM(cols.shape, jnp.int32),
            pltpu.SMEM((places,), jnp.int32),
            pltpu.SMEM((slots,), jnp.int32),
            pltpu.SMEM((slots + 1,), jnp.int32),
            pltpu.SMEM((slots + 1,), jnp.int32),
            pltpu.SemaphoreType.DMA,
            pltpu.SemaphoreType.DMA((2,)),
        ],
        compiler_params=pltpu.CompilerParams(vmem_limit_bytes=4 * 2**20),
        name="densify",
    )(
        pltpu.with_memory_space_constraint(rows, pltpu.HBM),
        pltpu.with_memory_space_constraint(cols, pltpu.HBM),
        count,
        pltpu.with_memory_space_constraint(values, pltpu.HBM),
    )


class Exchange:
    def __init__(self, axis, size, dst, send_sem, recv_sem):
        self.axis, self.size, self.dst = axis, size, dst
        self.send_sem, self.recv_sem = send_sem, recv_sem
        self.me = lax.axis_index(axis)

    def copy(self, source, target, peer):
        return pltpu.make_async_remote_copy(
            src_ref=source,
            dst_ref=target,
            send_sem=self.send_sem,
            recv_sem=self.recv_sem,
            device_id={self.axis: peer},
            device_id_type=MESH,
        )

    def peer(self, d):
        me, size = self.me, self.size
        if self.axis == "col":
            half = size // 2
            step = lax.rem(1 + d, half)
            return lax.rem(me // half + 1 - d // half, 2) * half + lax.rem(me + step, half)
        q = self.chip(lax.div(d, 2), 1)
        return 2 * q + lax.rem(me + 1 + d, 2)

    def chip(self, d, sign):
        q, half = self.me // 2, self.size // 4
        step = lax.rem(1 + d, half)
        return lax.rem(q // half + 1 - d // half, 2) * half + lax.rem(q + half + sign * step, half)

    def peers(self, body):
        def step(d, _):
            body(self.peer(d))
            return 0

        lax.fori_loop(0, self.size - 1, step, 0)

    def send(self, source, peer):
        self.copy(source, self.dst.at[self.me], peer).start()

    def send_all(self, source_of):
        self.peers(lambda peer: self.send(source_of(peer), peer))

    def everything(self):
        span = self.dst.at[pl.ds(0, self.size - 1)]
        return self.copy(span, span, lax.rem(self.me + 1, self.size))

    def receive_all(self):
        self.everything().wait_recv()

    def sent_all(self):
        self.everything().wait_send()


class Gather(Exchange):
    def copy(self, source, target, peer, slot=None):
        return pltpu.make_async_remote_copy(
            src_ref=source,
            dst_ref=target,
            send_sem=self.send_sem,
            recv_sem=self.recv_sem.at[self.me if slot is None else slot],
            device_id={self.axis: peer},
            device_id_type=MESH,
        )

    def receive(self, slot):
        self.copy(self.dst.at[slot], self.dst.at[slot], slot, slot).wait_recv()

    def by_chip(self, source, use):
        me, chips = self.me, self.size // 2
        own, core, half = me // 2, lax.rem(me, 2), self.size // 4
        beside = 2 * own + 1 - core

        def send(e, _):
            self.send(source, 2 * self.chip(chips - 2 - e, 1) + core)
            return 0

        def take(q):
            slot = 2 * q + core
            self.receive(slot)
            self.copy(self.dst.at[slot], self.dst.at[slot], beside, slot).start()

        def near(e, _):
            take(self.chip(chips - 2 - e, -1))
            return 0

        def near_other(e, _):
            self.receive(2 * self.chip(chips - 1 - e, -1) + 1 - core)
            return 0

        def far(e, _):
            take(self.chip(half - 1 - e, -1))
            use(self.chip(chips - 1 - e, -1))
            return 0

        def far_other(e, _):
            self.receive(2 * self.chip(half - 1 - e, -1) + 1 - core)
            return 0

        self.send(source, beside)
        lax.fori_loop(0, chips - 1, send, 0)
        lax.fori_loop(0, half - 1, near, 0)
        lax.fori_loop(0, half, near_other, 0)
        lax.fori_loop(0, half, far, 0)
        lax.fori_loop(0, half, far_other, 0)


def rows_of(dense, i, start, n_rows, n_cols):
    return jnp.concatenate(
        [
            dense[pl.ds((start + k) * n_rows + 2 * i, 2)].reshape(2 * TILE, TILE)
            for k in range(n_cols)
        ],
        axis=1,
    )


def cols_of(dense, q, n_rows):
    return jnp.concatenate(
        [
            dense[pl.ds((4 * q + h) * n_rows, n_rows)].reshape(n_rows * TILE, TILE)
            for h in range(4)
        ],
        axis=1,
    )


def add_up(ref, size):
    return lax.fori_loop(
        1, size, lambda j, total: total + ref[j].astype(jnp.float32), ref[0].astype(jnp.float32)
    )


def step_kernel(
    R,
    C,
    x,
    dense,
    labels,
    mask,
    w1,
    b1,
    w2,
    b2,
    hidden_out,
    logits_out,
    sums_out,
    xg,
    t1,
    r1,
    s2,
    hw,
    t2,
    r2,
    s3,
    gg,
    t3,
    r3,
    part,
    part16,
    r4,
    s5,
    r5,
    fin,
    first_acc,
    second_acc,
    pre,
    agg,
    w2s,
    b2s,
    send_sems,
    x_sems,
    hw_sems,
    recv_sems,
):
    n_rows, n_cols = 2 * C, 2 * R
    nodes = x.shape[0]
    classes = w2.shape[0]
    piece = fin.shape[1]
    row, col = lax.axis_index("row"), lax.axis_index("col")

    barrier = pltpu.get_barrier_semaphore()

    def greet(axis, me, size):
        def one(d, _):
            pl.semaphore_signal(
                barrier,
                inc=1,
                device_id={axis: lax.rem(me + d, size)},
                device_id_type=MESH,
            )
            return 0

        lax.fori_loop(1, size, one, 0)

    greet("row", row, R)
    greet("col", col, C)

    ex_x = Gather("row", R, xg, send_sems.at[0], x_sems)
    ex_first = Exchange("col", C, r1, send_sems.at[1], recv_sems.at[1])
    ex_hw = Gather("row", R, hw, send_sems.at[2], hw_sems)
    ex_second = Exchange("col", C, r2, send_sems.at[3], recv_sems.at[3])
    ex_grad = Exchange("col", C, gg, send_sems.at[4], recv_sems.at[4])
    ex_back = Exchange("row", R, r3, send_sems.at[5], recv_sems.at[5])
    ex_part = Exchange("col", C, r4, send_sems.at[6], recv_sems.at[6])
    ex_sum = Exchange("row", R, r5, send_sems.at[7], recv_sems.at[7])
    ex_fin = Exchange("col", C, fin, send_sems.at[8], recv_sems.at[8])

    xg[row] = x[...]
    w2s[...] = jnp.zeros_like(w2s)
    w2s[0:classes, :] = w2[...].astype(jnp.float32)
    b2s[...] = jnp.zeros_like(b2s)
    b2s[0:1, 0:classes] = b2[...]
    first_acc[...] = jnp.zeros_like(first_acc)
    second_acc[...] = jnp.zeros_like(second_acc)
    pl.semaphore_wait(barrier, R + C - 2)

    def use_x(q):
        first_acc[...] += jnp.dot(
            cols_of(dense, q, n_rows),
            xg[pl.ds(2 * q, 2)].reshape(2 * nodes, x.shape[1]),
            preferred_element_type=jnp.float32,
        )

    ex_x.by_chip(x, use_x)
    far = (R // 2) * (1 - row // (R // 2))

    def first(d, _):
        peer = ex_first.peer(d)
        rest = jnp.dot(
            rows_of(dense, peer, 2 * far, n_rows, R),
            xg[pl.ds(far, R // 2)].reshape(R // 2 * nodes, x.shape[1]),
            preferred_element_type=jnp.float32,
        )
        t1[peer] = (first_acc[pl.ds(peer * nodes, nodes), :] + rest).astype(t1.dtype)

        @pl.when(d < C - 1)
        def _():
            ex_first.send(t1.at[peer], peer)

        return 0

    lax.fori_loop(0, C, first, 0)
    r1[col] = t1[col]
    ex_first.receive_all()

    agg[...] = add_up(r1, C).astype(jnp.bfloat16)
    v = jnp.dot(agg[...], w1[...], preferred_element_type=jnp.float32) + b1[...]
    pre[...] = v
    hidden_out[...] = (v / (1.0 + jnp.exp(-v))).astype(jnp.bfloat16)
    s2[...] = lax.dot_general(
        w2s[...].astype(jnp.bfloat16), hidden_out[...], NT, preferred_element_type=jnp.float32
    ).astype(jnp.bfloat16)

    hw[row] = s2[...]
    def use_hw(q):
        second_acc[...] += lax.dot_general(
            jnp.concatenate([hw[2 * q], hw[2 * q + 1]], axis=1),
            cols_of(dense, q, n_rows),
            NT,
            preferred_element_type=jnp.float32,
        )

    ex_hw.by_chip(s2, use_hw)

    def second(d, _):
        peer = ex_second.peer(d)
        rest = lax.dot_general(
            jnp.concatenate([hw[far + k] for k in range(R // 2)], axis=1),
            rows_of(dense, peer, 2 * far, n_rows, R),
            NT,
            preferred_element_type=jnp.float32,
        )
        near = second_acc[:, pl.ds(pl.multiple_of(peer * nodes, nodes), nodes)]
        t2[peer] = (near + rest).astype(t2.dtype)

        @pl.when(d < C - 1)
        def _():
            ex_second.send(t2.at[peer], peer)

        return 0

    lax.fori_loop(0, C, second, 0)
    r2[col] = t2[col]
    ex_second.receive_all()

    turned = jnp.transpose(jnp.broadcast_to(b2s[0:1, :], (TILE, TILE)))[0:PADDED, :]
    logits = add_up(r2, C) + jnp.concatenate([turned] * (nodes // TILE), axis=1)
    logits_out[...] = logits[0:classes, :]
    index = lax.broadcasted_iota(jnp.int32, (PADDED, nodes), 0)
    real = index < classes
    top = jnp.max(jnp.where(real, logits, -jnp.inf), axis=0, keepdims=True)
    terms = jnp.where(real, jnp.exp(logits - top), 0.0)
    log_total = top + jnp.log(jnp.sum(terms, axis=0, keepdims=True))
    onehot = (index == labels[...]).astype(jnp.float32)
    weights = mask[...].astype(jnp.float32)
    cross = weights * (log_total - jnp.sum(onehot * logits, axis=0, keepdims=True))
    grad = jnp.where(real, jnp.exp(logits - log_total) - onehot, 0.0) * weights
    s3[...] = grad.astype(jnp.bfloat16)

    gg[col] = s3[...]
    ex_grad.send_all(lambda peer: s3)

    def halves(base, value):
        height = value.shape[0]
        for h in range(2):
            part[pl.ds(base + h * height, height), :] = value[:, h * TILE : (h + 1) * TILE]

    base2, base3 = 2 * w1.shape[0], 2 * w1.shape[0] + 2 * PADDED
    ones = jnp.ones((8, nodes), jnp.float32)
    b2_part = lax.dot_general(
        ones, grad, NT, precision=lax.Precision.HIGHEST, preferred_element_type=jnp.float32
    )
    part[pl.ds(base3, 32), :] = jnp.zeros((32, TILE), jnp.float32)
    part[pl.ds(base3 + 2, 1), 0:PADDED] = b2_part[0:1, :]
    part[pl.ds(base3 + 3, 1), :] = jnp.broadcast_to(
        jnp.sum(cross, axis=1, keepdims=True), (1, TILE)
    )
    part[pl.ds(base3 + 4, 1), :] = jnp.broadcast_to(
        jnp.sum(weights, axis=1, keepdims=True), (1, TILE)
    )

    ex_grad.receive_all()

    def back(d, _):
        q = ex_back.chip(d, 1)
        left = jnp.concatenate([gg[k] for k in range(C)], axis=1)
        both = jnp.dot(left, cols_of(dense, q, n_rows), preferred_element_type=jnp.float32)
        for h in range(2):
            t3[2 * q + h] = both[:, h * nodes : (h + 1) * nodes].astype(t3.dtype)

        @pl.when(d < R // 2 - 1)
        def _():
            for h in range(2):
                ex_back.send(t3.at[2 * q + h], 2 * q + h)

        return 0

    lax.fori_loop(0, R // 2, back, 0)
    beside = row + 1 - 2 * lax.rem(row, 2)
    ex_back.send(t3.at[beside], beside)
    r3[row] = t3[row]
    ex_back.receive_all()

    turned_grad = add_up(r3, R).astype(jnp.bfloat16)
    hidden_grad = lax.dot_general(
        turned_grad, w2s[...].astype(jnp.bfloat16), TN, preferred_element_type=jnp.float32
    )
    v = pre[...]
    s = 1.0 / (1.0 + jnp.exp(-v))
    pre_grad = hidden_grad * s * (1.0 + v * (1.0 - s))
    b1_part = jnp.sum(pre_grad, axis=0, keepdims=True)
    for h in range(2):
        part[pl.ds(base3 + h, 1), :] = b1_part[:, h * TILE : (h + 1) * TILE]
    halves(
        0,
        lax.dot_general(
            agg[...], pre_grad.astype(jnp.bfloat16), TN, preferred_element_type=jnp.float32
        ),
    )
    halves(
        base2,
        jnp.dot(turned_grad, hidden_out[...], preferred_element_type=jnp.float32),
    )

    def split(value):
        high = value.astype(jnp.bfloat16)
        return high, (value - high.astype(jnp.float32)).astype(jnp.bfloat16)

    last = C - 1
    part16[pl.ds(0, base3), :] = part[pl.ds(0, base3), :].astype(jnp.bfloat16)
    high, low = split(part[pl.ds(base3, 16), :])
    part16[pl.ds(base3, 16), :] = high
    part16[pl.ds(base3 + 16, 16), :] = low
    ex_part.send_all(
        lambda peer: part16.at[pl.ds(pl.multiple_of(peer * piece, piece), piece)]
    )
    r4[col] = part16[pl.ds(pl.multiple_of(col * piece, piece), piece), :]
    ex_part.receive_all()

    def resplit(total):
        high, low = split(total[piece - 32 : piece - 16, :] + total[piece - 16 :, :])
        both = jnp.concatenate([high, low], axis=0)
        plain = total.astype(jnp.bfloat16)
        tail = jnp.where(col == last, both, plain[piece - 32 :, :])
        return jnp.concatenate([plain[: piece - 32, :], tail], axis=0)

    s5[...] = resplit(add_up(r4, C))
    r5[row] = s5[...]
    ex_sum.send_all(lambda peer: s5)
    ex_sum.receive_all()

    fin[col] = resplit(add_up(r5, R))
    ex_fin.send_all(lambda peer: fin.at[col])
    ex_fin.receive_all()

    for j in range(C):
        sums_out[j * piece : (j + 1) * piece, :] = fin[j].astype(jnp.float32)
    for ex in (ex_first, ex_hw, ex_second, ex_grad, ex_back, ex_part, ex_sum, ex_fin):
        ex.sent_all()
    ex_x.sent_all()


def finish_kernel(
    features,
    classes,
    hidden,
    logits,
    sums,
    hidden_out,
    logits_out,
    loss_out,
    w1_grad_out,
    b1_grad_out,
    w2_grad_out,
    b2_grad_out,
    sems,
):
    copies = [
        pltpu.make_async_copy(hidden, hidden_out, sems.at[0]),
        pltpu.make_async_copy(logits, logits_out, sems.at[1]),
    ]
    for copy in copies:
        copy.start()
    base2, base3 = 2 * features, 2 * features + 2 * PADDED
    small = sums[base3 : base3 + 16, :] + sums[base3 + 16 : base3 + 32, :]
    count = small[4:5, 0:1]
    for h in range(2):
        lanes = slice(h * TILE, (h + 1) * TILE)
        w1_grad_out[:, lanes] = sums[h * features : (h + 1) * features, :] / count
        low = base2 + h * PADDED
        w2_grad_out[:, lanes] = sums[low : low + classes, :] / count
        b1_grad_out[:, lanes] = small[h : h + 1, :] / count
    b2_grad_out[...] = small[2:3, 0:classes] / count
    loss_out[...] = small[3:4, 0:1] / count
    for copy in copies:
        copy.wait()


def on_device(
    node_features,
    tile_values,
    tile_rows,
    tile_cols,
    tile_count,
    labels,
    train_mask,
    hidden_weight,
    hidden_bias,
    class_weight,
    class_bias,
):
    nodes, features = node_features.shape
    hidden, classes = class_weight.shape
    R, C = lax.axis_size("row"), lax.axis_size("col")
    n_rows, n_cols = C * nodes // TILE, R * nodes // TILE
    dense = densify(tile_rows, tile_cols, tile_count, tile_values[0, 0], n_rows, n_cols)
    used = 2 * features + 2 * PADDED + 32
    piece = used // C
    vmem = pl.BlockSpec(memory_space=pltpu.VMEM)
    hbm = pl.BlockSpec(memory_space=pltpu.HBM)
    bf16, f32 = jnp.bfloat16, jnp.float32
    out = lambda shape, kind: jax.ShapeDtypeStruct(shape, kind)
    scratch = [
        pltpu.VMEM((R, nodes, features), bf16),
        pltpu.VMEM((C, nodes, features), bf16),
        pltpu.VMEM((C, nodes, features), bf16),
        pltpu.VMEM((PADDED, nodes), bf16),
        pltpu.VMEM((R, PADDED, nodes), bf16),
        pltpu.VMEM((C, PADDED, nodes), bf16),
        pltpu.VMEM((C, PADDED, nodes), bf16),
        pltpu.VMEM((PADDED, nodes), bf16),
        pltpu.VMEM((C, PADDED, nodes), bf16),
        pltpu.VMEM((R, PADDED, nodes), bf16),
        pltpu.VMEM((R, PADDED, nodes), bf16),
        pltpu.VMEM((used, TILE), f32),
        pltpu.VMEM((used, TILE), bf16),
        pltpu.VMEM((C, piece, TILE), bf16),
        pltpu.VMEM((piece, TILE), bf16),
        pltpu.VMEM((R, piece, TILE), bf16),
        pltpu.VMEM((C, piece, TILE), bf16),
        pltpu.VMEM((C * nodes, features), f32),
        pltpu.VMEM((PADDED, C * nodes), f32),
        pltpu.VMEM((nodes, hidden), f32),
        pltpu.VMEM((nodes, features), bf16),
        pltpu.VMEM((PADDED, hidden), f32),
        pltpu.VMEM((8, TILE), f32),
        pltpu.SemaphoreType.DMA((9,)),
        pltpu.SemaphoreType.DMA((R,)),
        pltpu.SemaphoreType.DMA((R,)),
        pltpu.SemaphoreType.DMA((9,)),
    ]
    hidden_now, logits_now, sums = pl.pallas_call(
        lambda *refs: step_kernel(R, C, *refs),
        out_shape=(
            pltpu.VMEM((nodes, hidden), bf16),
            pltpu.VMEM((classes, nodes), f32),
            pltpu.VMEM((used, TILE), f32),
        ),
        in_specs=[vmem] * 8,
        out_specs=(vmem,) * 3,
        scratch_shapes=scratch,
        compiler_params=pltpu.CompilerParams(
            collective_id=0, has_side_effects=True, vmem_limit_bytes=24 * 2**20
        ),
        name="step",
    )(
        node_features,
        pltpu.with_memory_space_constraint(dense, pltpu.VMEM),
        labels.reshape(1, nodes),
        train_mask.reshape(1, nodes),
        hidden_weight,
        hidden_bias.reshape(1, hidden),
        class_weight.T,
        class_bias.reshape(1, classes),
    )
    hidden_out, logits, loss, w1_grad, b1_grad, w2_grad, b2_grad = pl.pallas_call(
        lambda *refs: finish_kernel(features, classes, *refs),
        out_shape=(
            out((nodes, hidden), bf16),
            out((classes, nodes), f32),
            out((1, 1), f32),
            out((features, hidden), f32),
            out((1, hidden), f32),
            out((classes, hidden), f32),
            out((1, classes), f32),
        ),
        in_specs=[vmem] * 3,
        out_specs=(hbm, hbm) + (vmem,) * 5,
        scratch_shapes=[pltpu.SemaphoreType.DMA((2,))],
        compiler_params=pltpu.CompilerParams(vmem_limit_bytes=4 * 2**20),
        name="finish",
    )(*(pltpu.with_memory_space_constraint(a, pltpu.VMEM) for a in (hidden_now, logits_now, sums)))
    return (
        hidden_out,
        logits,
        loss[0, 0],
        w1_grad,
        b1_grad[0],
        w2_grad.T,
        b2_grad[0],
    )


def solution(mesh):
    in_specs = (
        P(("row", "col"), None),
        P("row", "col", None, None, None),
        P("row", "col", None),
        P("row", "col", None),
        P("row", "col"),
        P(("row", "col")),
        P(("row", "col")),
        P(),
        P(),
        P(),
        P(),
    )
    out_specs = (P(("row", "col"), None), P(None, ("row", "col")), P(), P(), P(), P(), P())
    return jax.shard_map(
        on_device, mesh=mesh, in_specs=in_specs, out_specs=out_specs, check_vma=False
    )
```

```python
import jax
import jax.numpy as jnp
from jax import lax
from jax.experimental import pallas as pl
from jax.experimental.pallas import tpu as pltpu
from jax.sharding import PartitionSpec as P

TILE = 128
PADDED = 48
MESH = pl.DeviceIdType.MESH
NT = (((1,), (1,)), ((), ()))
TN = (((0,), (0,)), ((), ()))


def densify_kernel(n_rows, rows_in, cols_in, count, values, out, rows, cols, head, nxt, pairs, longer, sem, sems):
    slots = values.shape[0]
    places = head.shape[0]
    several = 1 << (slots - 1).bit_length()
    zero = jnp.zeros((TILE, TILE), jnp.bfloat16)
    loads = [
        pltpu.make_async_copy(source, target, sems.at[i])
        for i, (source, target) in enumerate(
            ((rows_in, rows), (cols_in, cols))
        )
    ]
    for load in loads:
        load.start()

    def clear(p, _):
        head[p] = -1
        out[p] = zero
        return 0

    lax.fori_loop(0, places, clear, 0, unroll=8)
    for load in loads:
        load.wait()
    live = count[0, 0]

    def place(s, found):
        seconds, more = found
        p = cols[0, 0, s] * n_rows + rows[0, 0, s]
        alive = s < live
        before = head[p]
        vacant = before < 0
        head[p] = jnp.where(alive, jnp.where(vacant, s, s + several), before)
        nxt[s] = before
        pairs[seconds] = p * several + s
        longer[more] = p
        pltpu.make_async_copy(
            values.at[s],
            out.at[jnp.where(jnp.logical_and(alive, vacant), p, places + s)],
            sem,
        ).start()
        third = jnp.logical_and(alive, before >= several)
        second = jnp.logical_and(alive, jnp.logical_and(before >= 0, before < several))
        return seconds + second.astype(jnp.int32), more + third.astype(jnp.int32)

    seconds, more = lax.fori_loop(0, slots, place, (0, 0), unroll=8)

    def slot_of(entry):
        return jnp.where(entry >= several, entry - several, entry)

    pltpu.make_async_copy(values, out.at[pl.ds(places, slots)], sem).wait()

    def merge(i, _):
        p = longer[i]
        top = slot_of(head[p])

        @pl.when(top >= 0)
        def _():
            head[p] = -1

            def going(state):
                return nxt[state[0]] >= 0

            def add(state):
                s, total = state
                tile = out[places + s].astype(jnp.float32)
                out[places + s] = zero
                return slot_of(nxt[s]), total + tile

            _, total = lax.while_loop(going, add, (top, out[p].astype(jnp.float32)))
            out[p] = total.astype(jnp.bfloat16)

        return 0

    lax.fori_loop(0, more, merge, 0)

    def add_second(i, _):
        sums = []
        for j in range(2):
            entry = jnp.where(2 * i + j < seconds, pairs[2 * i + j], places * several + slots)
            p = entry // several
            s = entry - p * several
            p = jnp.where(p == places, places + slots, p)
            total = out[p].astype(jnp.float32) + out[places + s].astype(jnp.float32)
            sums.append((p, total.astype(jnp.bfloat16)))
        for p, total in sums:
            out[p] = total
        return 0

    out[places + slots] = zero
    lax.fori_loop(0, (seconds + 1) // 2, add_second, 0)


def densify(rows, cols, count, values, n_rows, n_cols):
    slots = values.shape[0]
    places = n_rows * n_cols
    hbm = pl.BlockSpec(memory_space=pltpu.HBM)
    return pl.pallas_call(
        lambda *refs: densify_kernel(n_rows, *refs),
        out_shape=pltpu.VMEM((places + slots + 1, TILE, TILE), jnp.bfloat16),
        in_specs=[hbm, hbm, pl.BlockSpec(memory_space=pltpu.SMEM), hbm],
        out_specs=pl.BlockSpec(memory_space=pltpu.VMEM),
        scratch_shapes=[
            pltpu.SMEM(rows.shape, jnp.int32),
            pltpu.SMEM(cols.shape, jnp.int32),
            pltpu.SMEM((places,), jnp.int32),
            pltpu.SMEM((slots,), jnp.int32),
            pltpu.SMEM((slots + 2,), jnp.int32),
            pltpu.SMEM((slots + 1,), jnp.int32),
            pltpu.SemaphoreType.DMA,
            pltpu.SemaphoreType.DMA((2,)),
        ],
        compiler_params=pltpu.CompilerParams(vmem_limit_bytes=4 * 2**20),
        name="densify",
    )(
        pltpu.with_memory_space_constraint(rows, pltpu.HBM),
        pltpu.with_memory_space_constraint(cols, pltpu.HBM),
        count,
        pltpu.with_memory_space_constraint(values, pltpu.HBM),
    )


class Exchange:
    def __init__(self, axis, size, dst, send_sem, recv_sem):
        self.axis, self.size, self.dst = axis, size, dst
        self.send_sem, self.recv_sem = send_sem, recv_sem
        self.me = lax.axis_index(axis)

    def copy(self, source, target, peer):
        return pltpu.make_async_remote_copy(
            src_ref=source,
            dst_ref=target,
            send_sem=self.send_sem,
            recv_sem=self.recv_sem,
            device_id={self.axis: peer},
            device_id_type=MESH,
        )

    def peer(self, d):
        me, size = self.me, self.size
        if self.axis == "col":
            half = size // 2
            step = lax.rem(1 + d, half)
            return lax.rem(me // half + 1 - d // half, 2) * half + lax.rem(me + step, half)
        q = self.chip(lax.div(d, 2), 1)
        return 2 * q + lax.rem(me + 1 + d, 2)

    def chip(self, d, sign):
        q, half = self.me // 2, self.size // 4
        step = lax.rem(1 + d, half)
        return lax.rem(q // half + 1 - d // half, 2) * half + lax.rem(q + half + sign * step, half)

    def peers(self, body):
        def step(d, _):
            body(self.peer(d))
            return 0

        lax.fori_loop(0, self.size - 1, step, 0)

    def send(self, source, peer):
        self.copy(source, self.dst.at[self.me], peer).start()

    def send_all(self, source_of):
        self.peers(lambda peer: self.send(source_of(peer), peer))

    def everything(self):
        span = self.dst.at[pl.ds(0, self.size - 1)]
        return self.copy(span, span, lax.rem(self.me + 1, self.size))

    def receive_all(self):
        self.everything().wait_recv()

    def sent_all(self):
        self.everything().wait_send()


class Gather(Exchange):
    def copy(self, source, target, peer, slot=None):
        return pltpu.make_async_remote_copy(
            src_ref=source,
            dst_ref=target,
            send_sem=self.send_sem,
            recv_sem=self.recv_sem.at[self.me if slot is None else slot],
            device_id={self.axis: peer},
            device_id_type=MESH,
        )

    def receive(self, slot):
        self.copy(self.dst.at[slot], self.dst.at[slot], slot, slot).wait_recv()

    def by_chip(self, source, use):
        me, chips = self.me, self.size // 2
        own, core, half = me // 2, lax.rem(me, 2), self.size // 4
        beside = 2 * own + 1 - core

        def send(e, _):
            self.send(source, 2 * self.chip(chips - 2 - e, 1) + core)
            return 0

        def take(q):
            slot = 2 * q + core
            self.receive(slot)
            self.copy(self.dst.at[slot], self.dst.at[slot], beside, slot).start()

        def near(e, _):
            take(self.chip(chips - 2 - e, -1))
            return 0

        def near_other(e, _):
            self.receive(2 * self.chip(chips - 1 - e, -1) + 1 - core)
            return 0

        def far(e, _):
            take(self.chip(half - 1 - e, -1))
            use(self.chip(chips - 1 - e, -1))
            return 0

        def far_other(e, _):
            self.receive(2 * self.chip(half - 1 - e, -1) + 1 - core)
            return 0

        self.send(source, beside)
        lax.fori_loop(0, chips - 1, send, 0)
        lax.fori_loop(0, half - 1, near, 0)
        lax.fori_loop(0, half, near_other, 0)
        lax.fori_loop(0, half, far, 0)
        lax.fori_loop(0, half, far_other, 0)

    def direct(self, source, use):
        core, chips, half = lax.rem(self.me, 2), self.size // 2, self.size // 4

        def both(q):
            self.receive(2 * q)
            self.receive(2 * q + 1)

        def near(e, _):
            q = self.chip(chips - 1 - e, -1)
            both(q)
            use(q)
            return 0

        def far(e, _):
            both(self.chip(half - 1 - e, -1))
            return 0

        self.send_all(lambda peer: source)
        self.receive(2 * (self.me // 2) + 1 - core)
        use(self.me // 2)
        lax.fori_loop(1, half, near, 0)
        lax.fori_loop(0, half, far, 0)


def rows_of(dense, i, start, n_rows, n_cols):
    return jnp.concatenate(
        [
            dense[pl.ds((start + k) * n_rows + 2 * i, 2)].reshape(2 * TILE, TILE)
            for k in range(n_cols)
        ],
        axis=1,
    )


def cols_of(dense, q, n_rows):
    return jnp.concatenate(
        [
            dense[pl.ds((4 * q + h) * n_rows, n_rows)].reshape(n_rows * TILE, TILE)
            for h in range(4)
        ],
        axis=1,
    )


def add_up(ref, size):
    return lax.fori_loop(
        1, size, lambda j, total: total + ref[j].astype(jnp.float32), ref[0].astype(jnp.float32)
    )


def step_kernel(
    R,
    C,
    x,
    dense,
    labels,
    mask,
    w1,
    b1,
    w2,
    b2,
    hidden_out,
    logits_out,
    sums_out,
    xg,
    t1,
    r1,
    s2,
    hw,
    t2,
    r2,
    s3,
    gg,
    t3,
    r3,
    part,
    part16,
    r4,
    s5,
    r5,
    fin,
    first_acc,
    second_acc,
    pre,
    agg,
    w2s,
    b2s,
    send_sems,
    x_sems,
    hw_sems,
    recv_sems,
):
    n_rows, n_cols = 2 * C, 2 * R
    nodes = x.shape[0]
    classes = w2.shape[0]
    piece = fin.shape[1]
    row, col = lax.axis_index("row"), lax.axis_index("col")

    barrier = pltpu.get_barrier_semaphore()

    def greet(axis, me, size):
        def one(d, _):
            pl.semaphore_signal(
                barrier,
                inc=1,
                device_id={axis: lax.rem(me + d, size)},
                device_id_type=MESH,
            )
            return 0

        lax.fori_loop(1, size, one, 0)

    greet("row", row, R)
    greet("col", col, C)

    ex_x = Gather("row", R, xg, send_sems.at[0], x_sems)
    ex_first = Exchange("col", C, r1, send_sems.at[1], recv_sems.at[1])
    ex_hw = Gather("row", R, hw, send_sems.at[2], hw_sems)
    ex_second = Exchange("col", C, r2, send_sems.at[3], recv_sems.at[3])
    ex_grad = Exchange("col", C, gg, send_sems.at[4], recv_sems.at[4])
    ex_back = Exchange("row", R, r3, send_sems.at[5], recv_sems.at[5])
    ex_part = Exchange("col", C, r4, send_sems.at[6], recv_sems.at[6])
    ex_sum = Exchange("row", R, r5, send_sems.at[7], recv_sems.at[7])
    ex_fin = Exchange("col", C, fin, send_sems.at[8], recv_sems.at[8])

    xg[row] = x[...]
    w2s[...] = jnp.zeros_like(w2s)
    w2s[0:classes, :] = w2[...].astype(jnp.float32)
    b2s[...] = jnp.zeros_like(b2s)
    b2s[0:1, 0:classes] = b2[...]
    first_acc[...] = jnp.zeros_like(first_acc)
    second_acc[...] = jnp.zeros_like(second_acc)
    pl.semaphore_wait(barrier, R + C - 2)

    def use_x(q):
        first_acc[...] += jnp.dot(
            cols_of(dense, q, n_rows),
            xg[pl.ds(2 * q, 2)].reshape(2 * nodes, x.shape[1]),
            preferred_element_type=jnp.float32,
        )

    ex_x.by_chip(x, use_x)
    far = (R // 2) * (1 - row // (R // 2))

    def first(d, _):
        peer = ex_first.peer(d)
        rest = jnp.dot(
            rows_of(dense, peer, 2 * far, n_rows, R),
            xg[pl.ds(far, R // 2)].reshape(R // 2 * nodes, x.shape[1]),
            preferred_element_type=jnp.float32,
        )
        t1[peer] = (first_acc[pl.ds(peer * nodes, nodes), :] + rest).astype(t1.dtype)

        @pl.when(d < C - 1)
        def _():
            ex_first.send(t1.at[peer], peer)

        return 0

    lax.fori_loop(0, C, first, 0)
    r1[col] = t1[col]
    ex_first.receive_all()

    agg[...] = add_up(r1, C).astype(jnp.bfloat16)
    v = jnp.dot(agg[...], w1[...], preferred_element_type=jnp.float32) + b1[...]
    pre[...] = v
    hidden_out[...] = (v / (1.0 + jnp.exp(-v))).astype(jnp.bfloat16)
    s2[...] = lax.dot_general(
        w2s[...].astype(jnp.bfloat16), hidden_out[...], NT, preferred_element_type=jnp.float32
    ).astype(jnp.bfloat16)

    hw[row] = s2[...]
    def use_hw(q):
        second_acc[...] += lax.dot_general(
            jnp.concatenate([hw[2 * q], hw[2 * q + 1]], axis=1),
            cols_of(dense, q, n_rows),
            NT,
            preferred_element_type=jnp.float32,
        )

    ex_hw.direct(s2, use_hw)

    def second(d, _):
        peer = ex_second.peer(d)
        rest = lax.dot_general(
            jnp.concatenate([hw[far + k] for k in range(R // 2)], axis=1),
            rows_of(dense, peer, 2 * far, n_rows, R),
            NT,
            preferred_element_type=jnp.float32,
        )
        near = second_acc[:, pl.ds(pl.multiple_of(peer * nodes, nodes), nodes)]
        t2[peer] = (near + rest).astype(t2.dtype)

        @pl.when(d < C - 1)
        def _():
            ex_second.send(t2.at[peer], peer)

        return 0

    lax.fori_loop(0, C, second, 0)
    r2[col] = t2[col]
    ex_second.receive_all()

    turned = jnp.transpose(jnp.broadcast_to(b2s[0:1, :], (TILE, TILE)))[0:PADDED, :]
    logits = add_up(r2, C) + jnp.concatenate([turned] * (nodes // TILE), axis=1)
    logits_out[...] = logits[0:classes, :]
    index = lax.broadcasted_iota(jnp.int32, (PADDED, nodes), 0)
    real = index < classes
    top = jnp.max(jnp.where(real, logits, -jnp.inf), axis=0, keepdims=True)
    terms = jnp.where(real, jnp.exp(logits - top), 0.0)
    log_total = top + jnp.log(jnp.sum(terms, axis=0, keepdims=True))
    onehot = (index == labels[...]).astype(jnp.float32)
    weights = mask[...].astype(jnp.float32)
    cross = weights * (log_total - jnp.sum(onehot * logits, axis=0, keepdims=True))
    grad = jnp.where(real, jnp.exp(logits - log_total) - onehot, 0.0) * weights
    s3[...] = grad.astype(jnp.bfloat16)

    gg[col] = s3[...]
    ex_grad.send_all(lambda peer: s3)

    def halves(base, value):
        height = value.shape[0]
        for h in range(2):
            part[pl.ds(base + h * height, height), :] = value[:, h * TILE : (h + 1) * TILE]

    base2, base3 = 2 * w1.shape[0], 2 * w1.shape[0] + 2 * PADDED
    ones = jnp.ones((8, nodes), jnp.float32)
    b2_part = lax.dot_general(
        ones, grad, NT, precision=lax.Precision.HIGHEST, preferred_element_type=jnp.float32
    )
    part[pl.ds(base3, 32), :] = jnp.zeros((32, TILE), jnp.float32)
    part[pl.ds(base3 + 2, 1), 0:PADDED] = b2_part[0:1, :]
    part[pl.ds(base3 + 3, 1), :] = jnp.broadcast_to(
        jnp.sum(cross, axis=1, keepdims=True), (1, TILE)
    )
    part[pl.ds(base3 + 4, 1), :] = jnp.broadcast_to(
        jnp.sum(weights, axis=1, keepdims=True), (1, TILE)
    )

    ex_grad.receive_all()

    def back(d, _):
        q = ex_back.chip(d, 1)
        left = jnp.concatenate([gg[k] for k in range(C)], axis=1)
        both = jnp.dot(left, cols_of(dense, q, n_rows), preferred_element_type=jnp.float32)
        for h in range(2):
            t3[2 * q + h] = both[:, h * nodes : (h + 1) * nodes].astype(t3.dtype)

        @pl.when(d < R // 2 - 1)
        def _():
            for h in range(2):
                ex_back.send(t3.at[2 * q + h], 2 * q + h)

        return 0

    lax.fori_loop(0, R // 2, back, 0)
    beside = row + 1 - 2 * lax.rem(row, 2)
    ex_back.send(t3.at[beside], beside)
    r3[row] = t3[row]
    ex_back.receive_all()

    turned_grad = add_up(r3, R).astype(jnp.bfloat16)
    hidden_grad = lax.dot_general(
        turned_grad, w2s[...].astype(jnp.bfloat16), TN, preferred_element_type=jnp.float32
    )
    v = pre[...]
    s = 1.0 / (1.0 + jnp.exp(-v))
    pre_grad = hidden_grad * s * (1.0 + v * (1.0 - s))
    b1_part = jnp.sum(pre_grad, axis=0, keepdims=True)
    for h in range(2):
        part[pl.ds(base3 + h, 1), :] = b1_part[:, h * TILE : (h + 1) * TILE]
    halves(
        0,
        lax.dot_general(
            agg[...], pre_grad.astype(jnp.bfloat16), TN, preferred_element_type=jnp.float32
        ),
    )
    halves(
        base2,
        jnp.dot(turned_grad, hidden_out[...], preferred_element_type=jnp.float32),
    )

    def split(value):
        high = value.astype(jnp.bfloat16)
        return high, (value - high.astype(jnp.float32)).astype(jnp.bfloat16)

    last = C - 1
    part16[pl.ds(0, base3), :] = part[pl.ds(0, base3), :].astype(jnp.bfloat16)
    high, low = split(part[pl.ds(base3, 16), :])
    part16[pl.ds(base3, 16), :] = high
    part16[pl.ds(base3 + 16, 16), :] = low
    ex_part.send_all(
        lambda peer: part16.at[pl.ds(pl.multiple_of(peer * piece, piece), piece)]
    )
    r4[col] = part16[pl.ds(pl.multiple_of(col * piece, piece), piece), :]
    ex_part.receive_all()

    def resplit(total):
        high, low = split(total[piece - 32 : piece - 16, :] + total[piece - 16 :, :])
        both = jnp.concatenate([high, low], axis=0)
        plain = total.astype(jnp.bfloat16)
        tail = jnp.where(col == last, both, plain[piece - 32 :, :])
        return jnp.concatenate([plain[: piece - 32, :], tail], axis=0)

    s5[...] = resplit(add_up(r4, C))
    r5[row] = s5[...]
    ex_sum.send_all(lambda peer: s5)
    ex_sum.receive_all()

    fin[col] = resplit(add_up(r5, R))
    ex_fin.send_all(lambda peer: fin.at[col])
    ex_fin.receive_all()

    for j in range(C):
        sums_out[j * piece : (j + 1) * piece, :] = fin[j].astype(jnp.float32)
    for ex in (ex_first, ex_hw, ex_second, ex_grad, ex_back, ex_part, ex_sum, ex_fin):
        ex.sent_all()
    ex_x.sent_all()


def finish_kernel(
    features,
    classes,
    hidden,
    logits,
    sums,
    hidden_out,
    logits_out,
    loss_out,
    w1_grad_out,
    b1_grad_out,
    w2_grad_out,
    b2_grad_out,
    sems,
):
    copies = [
        pltpu.make_async_copy(hidden, hidden_out, sems.at[0]),
        pltpu.make_async_copy(logits, logits_out, sems.at[1]),
    ]
    for copy in copies:
        copy.start()
    base2, base3 = 2 * features, 2 * features + 2 * PADDED
    small = sums[base3 : base3 + 16, :] + sums[base3 + 16 : base3 + 32, :]
    count = small[4:5, 0:1]
    for h in range(2):
        lanes = slice(h * TILE, (h + 1) * TILE)
        w1_grad_out[:, lanes] = sums[h * features : (h + 1) * features, :] / count
        low = base2 + h * PADDED
        w2_grad_out[:, lanes] = sums[low : low + classes, :] / count
        b1_grad_out[:, lanes] = small[h : h + 1, :] / count
    b2_grad_out[...] = small[2:3, 0:classes] / count
    loss_out[...] = small[3:4, 0:1] / count
    for copy in copies:
        copy.wait()


def on_device(
    node_features,
    tile_values,
    tile_rows,
    tile_cols,
    tile_count,
    labels,
    train_mask,
    hidden_weight,
    hidden_bias,
    class_weight,
    class_bias,
):
    nodes, features = node_features.shape
    hidden, classes = class_weight.shape
    R, C = lax.axis_size("row"), lax.axis_size("col")
    n_rows, n_cols = C * nodes // TILE, R * nodes // TILE
    dense = densify(tile_rows, tile_cols, tile_count, tile_values[0, 0], n_rows, n_cols)
    used = 2 * features + 2 * PADDED + 32
    piece = used // C
    vmem = pl.BlockSpec(memory_space=pltpu.VMEM)
    hbm = pl.BlockSpec(memory_space=pltpu.HBM)
    bf16, f32 = jnp.bfloat16, jnp.float32
    out = lambda shape, kind: jax.ShapeDtypeStruct(shape, kind)
    scratch = [
        pltpu.VMEM((R, nodes, features), bf16),
        pltpu.VMEM((C, nodes, features), bf16),
        pltpu.VMEM((C, nodes, features), bf16),
        pltpu.VMEM((PADDED, nodes), bf16),
        pltpu.VMEM((R, PADDED, nodes), bf16),
        pltpu.VMEM((C, PADDED, nodes), bf16),
        pltpu.VMEM((C, PADDED, nodes), bf16),
        pltpu.VMEM((PADDED, nodes), bf16),
        pltpu.VMEM((C, PADDED, nodes), bf16),
        pltpu.VMEM((R, PADDED, nodes), bf16),
        pltpu.VMEM((R, PADDED, nodes), bf16),
        pltpu.VMEM((used, TILE), f32),
        pltpu.VMEM((used, TILE), bf16),
        pltpu.VMEM((C, piece, TILE), bf16),
        pltpu.VMEM((piece, TILE), bf16),
        pltpu.VMEM((R, piece, TILE), bf16),
        pltpu.VMEM((C, piece, TILE), bf16),
        pltpu.VMEM((C * nodes, features), f32),
        pltpu.VMEM((PADDED, C * nodes), f32),
        pltpu.VMEM((nodes, hidden), f32),
        pltpu.VMEM((nodes, features), bf16),
        pltpu.VMEM((PADDED, hidden), f32),
        pltpu.VMEM((8, TILE), f32),
        pltpu.SemaphoreType.DMA((9,)),
        pltpu.SemaphoreType.DMA((R,)),
        pltpu.SemaphoreType.DMA((R,)),
        pltpu.SemaphoreType.DMA((9,)),
    ]
    hidden_now, logits_now, sums = pl.pallas_call(
        lambda *refs: step_kernel(R, C, *refs),
        out_shape=(
            pltpu.VMEM((nodes, hidden), bf16),
            pltpu.VMEM((classes, nodes), f32),
            pltpu.VMEM((used, TILE), f32),
        ),
        in_specs=[vmem] * 8,
        out_specs=(vmem,) * 3,
        scratch_shapes=scratch,
        compiler_params=pltpu.CompilerParams(
            collective_id=0, has_side_effects=True, vmem_limit_bytes=24 * 2**20
        ),
        name="step",
    )(
        node_features,
        pltpu.with_memory_space_constraint(dense, pltpu.VMEM),
        labels.reshape(1, nodes),
        train_mask.reshape(1, nodes),
        hidden_weight,
        hidden_bias.reshape(1, hidden),
        class_weight.T,
        class_bias.reshape(1, classes),
    )
    hidden_out, logits, loss, w1_grad, b1_grad, w2_grad, b2_grad = pl.pallas_call(
        lambda *refs: finish_kernel(features, classes, *refs),
        out_shape=(
            out((nodes, hidden), bf16),
            out((classes, nodes), f32),
            out((1, 1), f32),
            out((features, hidden), f32),
            out((1, hidden), f32),
            out((classes, hidden), f32),
            out((1, classes), f32),
        ),
        in_specs=[vmem] * 3,
        out_specs=(hbm, hbm) + (vmem,) * 5,
        scratch_shapes=[pltpu.SemaphoreType.DMA((2,))],
        compiler_params=pltpu.CompilerParams(vmem_limit_bytes=4 * 2**20),
        name="finish",
    )(*(pltpu.with_memory_space_constraint(a, pltpu.VMEM) for a in (hidden_now, logits_now, sums)))
    return (
        hidden_out,
        logits,
        loss[0, 0],
        w1_grad,
        b1_grad[0],
        w2_grad.T,
        b2_grad[0],
    )


def solution(mesh):
    in_specs = (
        P(("row", "col"), None),
        P("row", "col", None, None, None),
        P("row", "col", None),
        P("row", "col", None),
        P("row", "col"),
        P(("row", "col")),
        P(("row", "col")),
        P(),
        P(),
        P(),
        P(),
    )
    out_specs = (P(("row", "col"), None), P(None, ("row", "col")), P(), P(), P(), P(), P())
    return jax.shard_map(
        on_device, mesh=mesh, in_specs=in_specs, out_specs=out_specs, check_vma=False
    )
```
